512 devices in a mesh: grid: 64 (over y, z), orb: 8 (over x, core).
Axes of the slice: x: 4, y: 4, z: 16, core: 2. Of those that a mesh axis runs over, the one named last changes fastest.
Arguments:
- orbitals: float32 [128, 32, 32, 1024], P('grid', None, None, 'orb'), may hold values from -14 to 14
- potential: float32 [128, 1024], P('grid'), may hold values from -1.5 to 0.5
Outputs:
- filtered: float32 [128, 32, 32, 1024], P('grid', None, None, 'orb')
- factor: float32 [1024, 1024], P(None, 'orb')
The draws below stay inside these ranges and needn't reach their ends.
All inputs are finite; a program needn't handle non-finite values.
Results may differ from the reference program's by a relative error of at most 0.00005.
Values sent between devices are 32-bit elements; how exact they have to be, the bound alone decides.
A program may use at most 64 MiB of HBM per device.

```python
import jax
import jax.numpy as jnp
from jax import lax

BLOCK = 128
DEGREE = 2
GX = 32
GY = 32
ORBITALS = 1024
NZ = 128
NPTS = 131072


def draw_orbitals(key, part):
    first_key = jax.random.fold_in(key, 0)
    shape = (NZ, GY, GX, ORBITALS)
    return jnp.clip(jax.random.normal(first_key, shape, jnp.float32), -4.0, 4.0)


def levels(key, dims, shards, low, top_value):
    loudness, own = 1.0, jax.random.fold_in(key, 6)
    for position, blocks in shards:
        draws = jnp.exp(jax.random.uniform(jax.random.fold_in(own, position), (blocks,), jnp.float32, low / len(shards), top_value / len(shards)))
        loudness = loudness * jnp.repeat(draws, dims[position] // blocks).reshape([-1 if axis == position else 1 for axis in range(len(dims))])
    return loudness


def setup_inputs(seed: int = 0) -> dict:
    seeds = jax.random.split(jax.random.key(seed), 3)
    orbitals = draw_orbitals(jax.random.fold_in(seeds[2], 71), 0)
    potential = jnp.clip(-1.5 + 2.0 * jax.random.uniform(seeds[1], (NZ, GY * GX), jnp.float32) ** levels(seeds[1], (NZ, GY * GX), ((0, 64),), -0.2, 0.2), -1.5, 0.5)
    return {"orbitals": orbitals, "potential": potential}


LOWER = 1.0
UPPER = 10.0
KINETIC = 0.5

def second_terms(wavefield, direction):
    near_sum = jnp.roll(wavefield, 1, direction) + jnp.roll(wavefield, -1, direction)
    far_sum = jnp.roll(wavefield, 2, direction) + jnp.roll(wavefield, -2, direction)
    return 2.5 * wavefield - 4.0 / 3.0 * near_sum + 1.0 / 12.0 * far_sum

def hamiltonian(wavefield, potential_grid):
    kinetic = second_terms(wavefield, 0) + second_terms(wavefield, 1) + second_terms(wavefield, 2)
    return KINETIC * kinetic + potential_grid[:, :, :, None] * wavefield

def chebyshev(orbital_block, potential_grid):
    centre = 0.5 * (UPPER + LOWER)
    half_width = 0.5 * (UPPER - LOWER)
    previous = orbital_block
    current = (hamiltonian(orbital_block, potential_grid) - centre * orbital_block) / half_width
    for iteration in range(DEGREE - 1):
        following = 2.0 * (hamiltonian(current, potential_grid) - centre * current) / half_width - previous
        previous, current = (current, following)
    return current

def reference(orbitals, potential):
    potential_grid = potential.reshape(NZ, GY, GX)
    block_count = ORBITALS // BLOCK
    orbital_blocks = jnp.moveaxis(orbitals.reshape(NZ, GY, GX, block_count, BLOCK), 3, 0)
    filtered_blocks = lax.map(lambda orbital_block: chebyshev(orbital_block, potential_grid), orbital_blocks)
    filtered = jnp.moveaxis(filtered_blocks, 0, 3).reshape(NZ, GY, GX, ORBITALS)
    correlation = jnp.einsum('zyxi,zyxj->ij', filtered.astype(jnp.float32), filtered.astype(jnp.float32), precision=lax.Precision.HIGHEST, preferred_element_type=jnp.float32) / NPTS
    lower_factor = jnp.linalg.cholesky(correlation)
    return (filtered, lower_factor.T)
```

```python
import functools

import jax
import jax.numpy as jnp
from jax import lax
from jax.experimental import pallas as pl
from jax.experimental.pallas import tpu as pltpu
from jax.sharding import PartitionSpec as P

GX = 32
GY = 32
LOWER = 1.0
UPPER = 10.0
KINETIC = 0.5

SIZE_X = 4
SIZE_Y = 4
SIZE_Z = 16
BLOCK = 128
BLOCKS = 8
KEPT = 5
ROWS = KEPT * BLOCK
PART_Y = ROWS // SIZE_Y
PART_Z = 16
OWNERS = PART_Y // PART_Z
TOTAL = BLOCK * BLOCKS

MESH = pl.DeviceIdType.MESH
HIGHEST = lax.Precision.HIGHEST


def factor_diagonal(work):
    sub = lax.broadcasted_iota(jnp.int32, (8, 128), 0)
    for p in range(16):
        o = 8 * p
        pl_ = work[o:o+8, 0:128]
        pr_ = work[o:o+8, 128:256]
        s = {}
        for i in range(8):
            for j in range(i, 8):
                s[i, j] = jnp.broadcast_to(pl_[i:i+1, o+j:o+j+1], (8, 128))
        r = [None]*8
        u = {}
        rows_l, rows_r = [], []
        L, R = pl_, pr_
        for k in range(8):
            r[k] = lax.rsqrt(s[k, k])
            for j in range(k+1, 8):
                u[k, j] = s[k, j] * r[k]
            for i in range(k+1, 8):
                for j in range(i, 8):
                    s[i, j] = s[i, j] - u[k, i] * u[k, j]
            kl = jnp.broadcast_to(L[k:k+1, :], (8, 128)) * r[k]
            kr = jnp.broadcast_to(R[k:k+1, :], (8, 128)) * r[k]
            rows_l.append(kl); rows_r.append(kr)
            if k < 7:
                col = u[k, 7]
                for i in range(6, k, -1):
                    col = jnp.where(sub == i, u[k, i], col)
                col = jnp.where(sub > k, col, 0.0)
                L = L - col * kl
                R = R - col * kr
        outl, outr = rows_l[7], rows_r[7]
        for k in range(6, -1, -1):
            outl = jnp.where(sub == k, rows_l[k], outl)
            outr = jnp.where(sub == k, rows_r[k], outr)
        work[o:o+8, 0:128] = outl
        work[o:o+8, 128:256] = outr
        for v in range(p+1, 16):
            a = 8 * v
            wl = work[a:a+8, 0:128]
            wr = work[a:a+8, 128:256]
            c = [jnp.broadcast_to(wl[:, o+k:o+k+1], (8, 128)) for k in range(8)]
            for k in range(8):
                c[k] = c[k] * r[k]
                for j in range(k+1, 8):
                    c[j] = c[j] - u[k, j] * c[k]
                wl = wl - c[k] * rows_l[k]
                wr = wr - c[k] * rows_r[k]
            work[a:a+8, 0:128] = wl
            work[a:a+8, 128:256] = wr


def block_place(row, column):
    if column - row < KEPT:
        return column, column - row
    return row, row - column + BLOCKS


def remote(src, dst, send, recv, device):
    return pltpu.make_async_remote_copy(
        src_ref=src, dst_ref=dst, send_sem=send, recv_sem=recv, device_id=device, device_id_type=MESH
    )


def factor_kernel(
    scale, part_ref, out_ref, from_y, from_z, summed, result, whole, work,
    send_y, recv_y, send_z, recv_z, send_gz, recv_gz, send_gy, recv_gy, send_x, recv_x, send_c, recv_c,
):
    g, b = lax.axis_index("grid"), lax.axis_index("orb")
    y, z = g // SIZE_Z, g % SIZE_Z
    x, core = b // 2, b % 2

    def at_y(d):
        return ((y + d) % SIZE_Y) * SIZE_Z + z, b

    def at_z(d):
        return y * SIZE_Z + (z + d) % SIZE_Z, b

    def at_x(d):
        return g, ((x + d) % SIZE_X) * 2 + core

    sibling = (g, x * 2 + 1 - core)

    barrier = pltpu.get_barrier_semaphore()
    for d in range(1, SIZE_Y):
        pl.semaphore_signal(barrier, inc=1, device_id=at_y(d), device_id_type=MESH)
    for d in range(1, SIZE_Z):
        pl.semaphore_signal(barrier, inc=1, device_id=at_z(d), device_id_type=MESH)
    for d in range(1, SIZE_X):
        pl.semaphore_signal(barrier, inc=1, device_id=at_x(d), device_id_type=MESH)
    pl.semaphore_signal(barrier, inc=1, device_id=sibling, device_id_type=MESH)
    pl.semaphore_wait(barrier, SIZE_Y + SIZE_Z + SIZE_X - 2)

    copies = []
    for d in range(1, SIZE_Y):
        there = (y + d) % SIZE_Y
        copies.append(remote(part_ref.at[pl.ds(there * PART_Y, PART_Y)], from_y.at[d - 1], send_y.at[d - 1], recv_y.at[d - 1], at_y(d)))
        copies[-1].start()
    for c in copies:
        c.wait_recv()
    summed[...] = part_ref[pl.ds(y * PART_Y, PART_Y), :] + from_y[0] + from_y[1] + from_y[2]

    for d in range(1, SIZE_Z):
        there = (z + d) % SIZE_Z

        @pl.when(there < OWNERS)
        def _():
            remote(summed.at[pl.ds(there * PART_Z, PART_Z)], from_z.at[d - 1], send_z.at[d - 1], recv_z.at[d - 1], at_z(d)).start()

    mine = result.at[b]

    @pl.when(z < OWNERS)
    def _():
        for d in range(1, SIZE_Z):
            remote(summed.at[pl.ds(0, PART_Z)], from_z.at[d - 1], send_z.at[d - 1], recv_z.at[d - 1], at_z(d)).wait_recv()
        total = summed[pl.ds(z * PART_Z, PART_Z), :]
        for d in range(1, SIZE_Z):
            total = total + from_z[d - 1]
        place = pl.ds(y * PART_Y + z * PART_Z, PART_Z)
        result[b, place, :] = total * scale
        for d in range(1, SIZE_Z):
            remote(mine.at[place], mine.at[place], send_gz.at[d - 1], recv_gz.at[d - 1], at_z(d)).start()

    for d in range(1, SIZE_Z):
        source = (z + SIZE_Z - d) % SIZE_Z

        @pl.when(source < OWNERS)
        def _():
            place = pl.ds(y * PART_Y + source * PART_Z, PART_Z)
            remote(mine.at[place], mine.at[place], send_gz.at[d - 1], recv_gz.at[d - 1], at_z(d)).wait_recv()

    for d in range(1, SIZE_Y):
        place = pl.ds(y * PART_Y, PART_Y)
        remote(mine.at[place], mine.at[place], send_gy.at[d - 1], recv_gy.at[d - 1], at_y(d)).start()
    for d in range(1, SIZE_Y):
        place = pl.ds(((y + SIZE_Y - d) % SIZE_Y) * PART_Y, PART_Y)
        remote(mine.at[place], mine.at[place], send_gy.at[d - 1], recv_gy.at[d - 1], at_y(d)).wait_recv()

    for d in range(1, SIZE_X):
        remote(mine, mine, send_x.at[d - 1], recv_x.at[d - 1], at_x(d)).start()
    remote(mine, mine, send_c.at[0], recv_c.at[0], sibling).start()
    for d in range(1, SIZE_X):
        other = ((x + SIZE_X - d) % SIZE_X) * 2 + core
        remote(result.at[other], result.at[other], send_x.at[d - 1], recv_x.at[d - 1], at_x(d)).wait_recv()
        remote(result.at[other], result.at[other], send_c.at[d], recv_c.at[d], sibling).start()
    for d in range(SIZE_X):
        other = ((x + SIZE_X - d) % SIZE_X) * 2 + 1 - core
        remote(result.at[other], result.at[other], send_c.at[d], recv_c.at[d], sibling).wait_recv()

    for i in range(BLOCKS):
        for j in range(i, BLOCKS):
            owner, place = block_place(i, j)
            whole[i * BLOCK : (i + 1) * BLOCK, j * BLOCK : (j + 1) * BLOCK] = result[owner, place * BLOCK : (place + 1) * BLOCK, :]

    cholesky(whole, work)
    out_ref[...] = whole[:, pl.ds(pl.multiple_of(b * BLOCK, BLOCK), BLOCK)]

    for d in range(1, SIZE_Y):
        remote(from_y.at[0], from_y.at[0], send_y.at[d - 1], recv_y.at[d - 1], at_y(d)).wait_send()
        remote(mine.at[pl.ds(0, PART_Y)], mine.at[pl.ds(0, PART_Y)], send_gy.at[d - 1], recv_gy.at[d - 1], at_y(d)).wait_send()
    for d in range(1, SIZE_Z):
        there = (z + d) % SIZE_Z

        @pl.when(there < OWNERS)
        def _():
            remote(from_z.at[0], from_z.at[0], send_z.at[d - 1], recv_z.at[d - 1], at_z(d)).wait_send()

        @pl.when(z < OWNERS)
        def _():
            remote(from_z.at[0], from_z.at[0], send_gz.at[d - 1], recv_gz.at[d - 1], at_z(d)).wait_send()

    for d in range(1, SIZE_X):
        remote(mine, mine, send_x.at[d - 1], recv_x.at[d - 1], at_x(d)).wait_send()
    for d in range(SIZE_X):
        remote(mine, mine, send_c.at[d], recv_c.at[d], sibling).wait_send()


def cholesky(S, work):
    row = lax.broadcasted_iota(jnp.int32, (BLOCK, BLOCK), 0)
    column = lax.broadcasted_iota(jnp.int32, (BLOCK, BLOCK), 1)

    def step(k, carry):
        for kk in range(BLOCKS):

            @pl.when(k == kk)
            def _():
                work[:, 0:BLOCK] = S[kk * BLOCK : (kk + 1) * BLOCK, kk * BLOCK : (kk + 1) * BLOCK]

        work[:, BLOCK:] = jnp.where(row == column, 1.0, 0.0)
        factor_diagonal(work)
        for kk in range(BLOCKS):

            @pl.when(k == kk)
            def _():
                lo, hi = kk * BLOCK, (kk + 1) * BLOCK
                S[lo:hi, lo:hi] = jnp.where(column >= row, work[:, 0:BLOCK], 0.0)
                if kk < BLOCKS - 1:
                    inverse = jnp.where(column <= row, work[:, BLOCK:], 0.0)
                    S[lo:hi, hi:] = jnp.dot(inverse, S[lo:hi, hi:], precision=HIGHEST, preferred_element_type=jnp.float32)
                    for a in range(kk + 1, BLOCKS):
                        left = S[lo:hi, a * BLOCK : (a + 1) * BLOCK]
                        S[a * BLOCK : (a + 1) * BLOCK, a * BLOCK :] -= lax.dot_general(
                            left, S[lo:hi, a * BLOCK :], (((0,), (0,)), ((), ())),
                            precision=HIGHEST, preferred_element_type=jnp.float32,
                        )

        return carry

    lax.fori_loop(0, BLOCKS, step, 0)
    for a in range(1, BLOCKS):
        S[a * BLOCK : (a + 1) * BLOCK, 0 : a * BLOCK] = jnp.zeros((BLOCK, a * BLOCK), jnp.float32)


def summed_factor(part, cells):
    dma = pltpu.SemaphoreType.DMA
    return pl.pallas_call(
        functools.partial(factor_kernel, 1.0 / cells),
        out_shape=jax.ShapeDtypeStruct((TOTAL, BLOCK), jnp.float32),
        in_specs=[pl.BlockSpec(memory_space=pltpu.VMEM)],
        out_specs=pl.BlockSpec(memory_space=pltpu.VMEM),
        scratch_shapes=[
            pltpu.VMEM((SIZE_Y - 1, PART_Y, BLOCK), jnp.float32),
            pltpu.VMEM((SIZE_Z - 1, PART_Z, BLOCK), jnp.float32),
            pltpu.VMEM((PART_Y, BLOCK), jnp.float32),
            pltpu.VMEM((BLOCKS, ROWS, BLOCK), jnp.float32),
            pltpu.VMEM((TOTAL, TOTAL), jnp.float32),
            pltpu.VMEM((BLOCK, 2 * BLOCK), jnp.float32),
            dma((SIZE_Y - 1,)), dma((SIZE_Y - 1,)),
            dma((SIZE_Z - 1,)), dma((SIZE_Z - 1,)),
            dma((SIZE_Z - 1,)), dma((SIZE_Z - 1,)),
            dma((SIZE_Y - 1,)), dma((SIZE_Y - 1,)),
            dma((SIZE_X - 1,)), dma((SIZE_X - 1,)),
            dma((SIZE_X,)), dma((SIZE_X,)),
        ],
        compiler_params=pltpu.CompilerParams(
            collective_id=1, has_side_effects=True, vmem_limit_bytes=40 * 1024 * 1024
        ),
        name="summed_factor",
    )(part)


def padded_2(value, sides, width):
    for axis, dim in sides:
        devices, length = (lax.axis_size(axis), value.shape[dim])
        up = [(i, (i + 1) % devices) for i in range(devices)]
        down = [(j, i) for i, j in up]
        last = lax.slice_in_dim(value, length - width, length, axis=dim)
        initial = lax.slice_in_dim(value, 0, width, axis=dim)
        before = lax.ppermute(last, axis, up)
        after = lax.ppermute(initial, axis, down)
        value = jnp.concatenate([before, value, after], axis=dim)
    return value


def plane_terms(wavefield, direction):
    near_sum = jnp.roll(wavefield, 1, direction) + jnp.roll(wavefield, -1, direction)
    far_sum = jnp.roll(wavefield, 2, direction) + jnp.roll(wavefield, -2, direction)
    return 2.5 * wavefield - 4.0 / 3.0 * near_sum + 1.0 / 12.0 * far_sum


def apply_operator(wavefield, potential_grid):
    padded = padded_2(wavefield, (("grid", 0),), 2)
    layers = wavefield.shape[0]
    near_sum = padded[3 : layers + 3] + padded[1 : layers + 1]
    far_sum = padded[4 : layers + 4] + padded[0:layers]
    depth_terms = 2.5 * wavefield - 4.0 / 3.0 * near_sum + 1.0 / 12.0 * far_sum
    kinetic = depth_terms + plane_terms(wavefield, 1) + plane_terms(wavefield, 2)
    return KINETIC * kinetic + potential_grid[:, :, :, None] * wavefield


def pair_product(left_block, right_block):
    return jnp.einsum(
        "zyxi,zyxj->ij",
        left_block,
        right_block,
        precision=lax.Precision.HIGHEST,
        preferred_element_type=jnp.float32,
    )


def local(orbitals, potential):
    potential_grid = potential.reshape(orbitals.shape[0], GY, GX)
    centre = 0.5 * (UPPER + LOWER)
    half_width = 0.5 * (UPPER - LOWER)
    previous = orbitals
    current = (apply_operator(orbitals, potential_grid) - centre * orbitals) / half_width
    following = (
        2.0 * (apply_operator(current, potential_grid) - centre * current) / half_width - previous
    )
    previous, current = (current, following)
    width = current.shape[3]
    block_count = lax.axis_size("orb")
    own_index = lax.axis_index("orb")
    cells = current.shape[0] * current.shape[1] * current.shape[2] * lax.axis_size("grid")
    column = pair_product(lax.all_gather(current, "orb", axis=3, tiled=True), current)
    column = column.reshape(block_count, width, width)
    parts = []
    for j in range(KEPT):
        block = lax.dynamic_index_in_dim(column, (own_index - j) % block_count, 0, keepdims=False)
        parts.append(jnp.where(own_index >= j, block, block.T))
    factor_block = summed_factor(jnp.concatenate(parts, axis=0), cells)
    return (current, factor_block)


def solution(mesh):
    placed = (P("grid", None, None, "orb"), P("grid", None))
    return jax.shard_map(
        local,
        mesh=mesh,
        in_specs=placed,
        out_specs=(P("grid", None, None, "orb"), P(None, "orb")),
        check_vma=False,
    )
```

```python
import functools

import jax
import jax.numpy as jnp
from jax import lax
from jax.experimental import pallas as pl
from jax.experimental.pallas import tpu as pltpu
from jax.sharding import PartitionSpec as P

GX = 32
GY = 32
LOWER = 1.0
UPPER = 10.0
KINETIC = 0.5
CENTRE = 0.5 * (UPPER + LOWER)
HALF_WIDTH = 0.5 * (UPPER - LOWER)

SIZE_X = 4
SIZE_Y = 4
SIZE_Z = 16
BLOCK = 128
BLOCKS = 8
KEPT = 5
ROWS = KEPT * BLOCK
PART_Y = ROWS // SIZE_Y
PART_Z = 16
OWNERS = PART_Y // PART_Z
TOTAL = BLOCK * BLOCKS

CHUNKS = tuple((4 * i, 4) for i in range(7)) + ((28, 2), (30, 2))
AHEAD = 3

MESH = pl.DeviceIdType.MESH
HIGHEST = lax.Precision.HIGHEST


def factor_diagonal(work):
    sub = lax.broadcasted_iota(jnp.int32, (8, 128), 0)
    for p in range(16):
        o = 8 * p
        pl_ = work[o:o+8, 0:128]
        pr_ = work[o:o+8, 128:256]
        s = {}
        for i in range(8):
            for j in range(i, 8):
                s[i, j] = jnp.broadcast_to(pl_[i:i+1, o+j:o+j+1], (8, 128))
        r = [None]*8
        u = {}
        rows_l, rows_r = [], []
        L, R = pl_, pr_
        for k in range(8):
            r[k] = lax.rsqrt(s[k, k])
            for j in range(k+1, 8):
                u[k, j] = s[k, j] * r[k]
            for i in range(k+1, 8):
                for j in range(i, 8):
                    s[i, j] = s[i, j] - u[k, i] * u[k, j]
            kl = jnp.broadcast_to(L[k:k+1, :], (8, 128)) * r[k]
            kr = jnp.broadcast_to(R[k:k+1, :], (8, 128)) * r[k]
            rows_l.append(kl); rows_r.append(kr)
            if k < 7:
                col = u[k, 7]
                for i in range(6, k, -1):
                    col = jnp.where(sub == i, u[k, i], col)
                col = jnp.where(sub > k, col, 0.0)
                L = L - col * kl
                R = R - col * kr
        outl, outr = rows_l[7], rows_r[7]
        for k in range(6, -1, -1):
            outl = jnp.where(sub == k, rows_l[k], outl)
            outr = jnp.where(sub == k, rows_r[k], outr)
        work[o:o+8, 0:128] = outl
        work[o:o+8, 128:256] = outr
        for v in range(p+1, 16):
            a = 8 * v
            wl = work[a:a+8, 0:128]
            wr = work[a:a+8, 128:256]
            c = [jnp.broadcast_to(wl[:, o+k:o+k+1], (8, 128)) for k in range(8)]
            for k in range(8):
                c[k] = c[k] * r[k]
                for j in range(k+1, 8):
                    c[j] = c[j] - u[k, j] * c[k]
                wl = wl - c[k] * rows_l[k]
                wr = wr - c[k] * rows_r[k]
            work[a:a+8, 0:128] = wl
            work[a:a+8, 128:256] = wr


def block_place(row, column):
    if column - row < KEPT:
        return row, column - row
    return column, row - column + BLOCKS


def remote(src, dst, send, recv, device):
    return pltpu.make_async_remote_copy(
        src_ref=src, dst_ref=dst, send_sem=send, recv_sem=recv, device_id=device, device_id_type=MESH
    )


def add_slab(source, before, after, weight, y):
    rows = [source[layer, y] for layer in range(2)]
    scale = KINETIC / HALF_WIDTH
    out = []
    for layer in range(2):
        own = rows[layer]
        if layer == 0:
            near = rows[1] + before[1, y]
            far = before[0, y] + after[0, y]
        else:
            near = rows[0] + after[0, y]
            far = before[1, y] + after[1, y]
        near = near + (source[layer, (y + GY - 1) % GY] + source[layer, (y + 1) % GY])
        far = far + (source[layer, (y + GY - 2) % GY] + source[layer, (y + 2) % GY])
        near = near + (pltpu.roll(own, 1, 0) + pltpu.roll(own, GX - 1, 0))
        far = far + (pltpu.roll(own, 2, 0) + pltpu.roll(own, GX - 2, 0))
        out.append(weight[layer, y] * own - (4.0 / 3.0 * scale) * near + (1.0 / 12.0 * scale) * far)
    return out


def factor_kernel(
    scale, orbitals_ref, potential_ref, filtered_ref, out_ref,
    weight, slab, before, after, current, before_2, after_2, filtered, gathered, relay, part,
    from_y, from_z, summed, result, whole, work,
    local_sem, send_h, recv_h, send_k, recv_k, send_o, recv_o, send_s, recv_s,
    send_y, recv_y, send_z, recv_z, send_gz, recv_gz, send_gy, recv_gy, send_x, recv_x, send_c, recv_c,
):
    g, b = lax.axis_index("grid"), lax.axis_index("orb")
    y, z = g // SIZE_Z, g % SIZE_Z
    x, core = b // 2, b % 2
    slabs = SIZE_Y * SIZE_Z
    ahead, behind = ((g + 1) % slabs, b), ((g + slabs - 1) % slabs, b)
    count = len(CHUNKS)

    def at_y(d):
        return ((y + d) % SIZE_Y) * SIZE_Z + z, b

    def at_z(d):
        return y * SIZE_Z + (z + d) % SIZE_Z, b

    def at_x(d):
        return g, ((x + d) % SIZE_X) * 2 + core

    sibling = (g, x * 2 + 1 - core)

    barrier = pltpu.get_barrier_semaphore()
    for device in (ahead, behind):
        pl.semaphore_signal(barrier, inc=1, device_id=device, device_id_type=MESH)
    for d in range(1, SIZE_X):
        pl.semaphore_signal(barrier, inc=1, device_id=at_x(d), device_id_type=MESH)
    pl.semaphore_signal(barrier, inc=1, device_id=sibling, device_id_type=MESH)
    for d in range(1, SIZE_Y):
        pl.semaphore_signal(barrier, inc=1, device_id=at_y(d), device_id_type=MESH)
    for d in range(1, SIZE_Z):
        pl.semaphore_signal(barrier, inc=1, device_id=at_z(d), device_id_type=MESH)
    load = pltpu.make_async_copy(orbitals_ref, slab, local_sem.at[0])
    load.start()
    pl.semaphore_wait(barrier, SIZE_Y + SIZE_Z + SIZE_X)

    def rows(k):
        return pl.ds(CHUNKS[k][0], CHUNKS[k][1])

    def halo(source, low, high, send, recv, k):
        return (
            remote(source.at[:, rows(k)], low.at[:, rows(k)], send.at[0, k], recv.at[0, k], ahead),
            remote(source.at[:, rows(k)], high.at[:, rows(k)], send.at[1, k], recv.at[1, k], behind),
        )

    def first_halo(k):
        return halo(orbitals_ref, before, after, send_h, recv_h, k)

    def second_halo(k):
        return halo(current, before_2, after_2, send_k, recv_k, k)

    def to_left(k):
        return remote(filtered.at[:, rows(k)], gathered.at[1, :, rows(k)], send_o.at[0, k], recv_o.at[0, k], at_x(SIZE_X - 1))

    def to_right(k):
        return remote(filtered.at[1, rows(k)], relay.at[rows(k)], send_o.at[1, k], recv_o.at[1, k], at_x(1))

    def on_left(k):
        return remote(gathered.at[1, 0, rows(k)], gathered.at[3, 0, rows(k)], send_o.at[2, k], recv_o.at[2, k], at_x(SIZE_X - 1))

    def on_right(k):
        return remote(relay.at[rows(k)], gathered.at[3, 1, rows(k)], send_o.at[3, k], recv_o.at[3, k], at_x(1))

    def across(source, slot, k):
        return remote(source.at[:, rows(k)], gathered.at[2 * slot, :, rows(k)], send_s.at[slot, k], recv_s.at[slot, k], sibling)

    def store(k):
        return pltpu.make_async_copy(filtered.at[:, rows(k)], filtered_ref.at[:, rows(k)], local_sem.at[1 + k])

    for k in range(AHEAD):
        for copy in first_halo(k):
            copy.start()

    table = potential_ref[...]
    for i in range(2 * GY):
        weight[i // GY, i % GY] = (jnp.broadcast_to(table[:, i : i + 1], (GX, BLOCK)) + (7.5 * KINETIC - CENTRE)) * (1.0 / HALF_WIDTH)
    part[...] = jnp.zeros_like(part)
    load.wait()

    def first_step(k):
        for copy in first_halo(k):
            copy.wait_recv()
        start, height = CHUNKS[k]

        def line(i, carry):
            for layer, value in enumerate(add_slab(slab, before, after, weight, start + i)):
                current[layer, start + i] = value
            return carry

        lax.fori_loop(0, height, line, 0)
        for copy in second_halo(k):
            copy.start()
        if k + AHEAD < count:
            for copy in first_halo(k + AHEAD):
                copy.start()

    def second_step(k):
        for copy in second_halo(k):
            copy.wait_recv()
        start, height = CHUNKS[k]

        def line(i, carry):
            for layer, value in enumerate(add_slab(current, before_2, after_2, weight, start + i)):
                filtered[layer, start + i] = 2.0 * value - slab[layer, start + i]
            return carry

        lax.fori_loop(0, height, line, 0)
        to_left(k).start()
        to_right(k).start()

        @pl.when(core == 1)
        def _():
            across(filtered, 0, k).start()

        store(k).start()

    def pass_on(k):
        to_left(k).wait_recv()
        on_left(k).start()
        to_right(k).wait_recv()
        on_right(k).start()

        @pl.when(core == 1)
        def _():
            across(gathered.at[1], 1, k).start()

        @pl.when(core == 0)
        def _():
            across(gathered.at[1], 0, k).start()

    def share(k):
        on_left(k).wait_recv()
        on_right(k).wait_recv()

        @pl.when(core == 0)
        def _():
            across(gathered.at[3], 1, k).start()

    def multiply(k):
        across(filtered, 0, k).wait_recv()
        across(filtered, 1, k).wait_recv()
        cells = 2 * CHUNKS[k][1] * GX
        own = filtered[:, rows(k)].reshape(cells, BLOCK)
        others = [own] + [gathered[j, :, rows(k)].reshape(cells, BLOCK) for j in range(KEPT - 1)]
        product = lax.dot_general(
            own, jnp.concatenate(others, axis=1), (((0,), (0,)), ((), ())),
            precision=HIGHEST, preferred_element_type=jnp.float32,
        )
        for j in range(KEPT):
            part[j * BLOCK : (j + 1) * BLOCK, :] += product[:, j * BLOCK : (j + 1) * BLOCK]

    stages = (second_step, pass_on, share, multiply)
    order = []

    def advance(k):
        order.append(k)
        for lag, stage in enumerate(stages):
            place = len(order) - 1 - lag
            if 0 <= place < count and order[place] is not None:
                stage(order[place])

    for k in range(count):
        first_step(k)
        if k - AHEAD >= 1:
            advance(k - AHEAD)
    advance(0)
    for k in range(count - AHEAD, count):
        advance(k)
    for lag in range(1, len(stages)):
        advance(None)

    for j in range(1, KEPT):

        @pl.when(b + j >= BLOCKS)
        def _():
            part[j * BLOCK : (j + 1) * BLOCK, :] = part[j * BLOCK : (j + 1) * BLOCK, :].T

    copies = []
    for d in range(1, SIZE_Y):
        there = (y + d) % SIZE_Y
        copies.append(remote(part.at[pl.ds(there * PART_Y, PART_Y)], from_y.at[d - 1], send_y.at[d - 1], recv_y.at[d - 1], at_y(d)))
        copies[-1].start()
    for c in copies:
        c.wait_recv()
    summed[...] = part[pl.ds(y * PART_Y, PART_Y), :] + from_y[0] + from_y[1] + from_y[2]

    for d in range(1, SIZE_Z):
        there = (z + d) % SIZE_Z

        @pl.when(there < OWNERS)
        def _():
            remote(summed.at[pl.ds(there * PART_Z, PART_Z)], from_z.at[d - 1], send_z.at[d - 1], recv_z.at[d - 1], at_z(d)).start()

    mine = result.at[b]

    @pl.when(z < OWNERS)
    def _():
        for d in range(1, SIZE_Z):
            remote(summed.at[pl.ds(0, PART_Z)], from_z.at[d - 1], send_z.at[d - 1], recv_z.at[d - 1], at_z(d)).wait_recv()
        total = summed[pl.ds(z * PART_Z, PART_Z), :]
        for d in range(1, SIZE_Z):
            total = total + from_z[d - 1]
        place = pl.ds(y * PART_Y + z * PART_Z, PART_Z)
        result[b, place, :] = total * scale
        for d in range(1, SIZE_Z):
            remote(mine.at[place], mine.at[place], send_gz.at[d - 1], recv_gz.at[d - 1], at_z(d)).start()

    for d in range(1, SIZE_Z):
        source = (z + SIZE_Z - d) % SIZE_Z

        @pl.when(source < OWNERS)
        def _():
            place = pl.ds(y * PART_Y + source * PART_Z, PART_Z)
            remote(mine.at[place], mine.at[place], send_gz.at[d - 1], recv_gz.at[d - 1], at_z(d)).wait_recv()

    for d in range(1, SIZE_Y):
        place = pl.ds(y * PART_Y, PART_Y)
        remote(mine.at[place], mine.at[place], send_gy.at[d - 1], recv_gy.at[d - 1], at_y(d)).start()
    for d in range(1, SIZE_Y):
        place = pl.ds(((y + SIZE_Y - d) % SIZE_Y) * PART_Y, PART_Y)
        remote(mine.at[place], mine.at[place], send_gy.at[d - 1], recv_gy.at[d - 1], at_y(d)).wait_recv()

    for d in range(1, SIZE_X):
        remote(mine, mine, send_x.at[d - 1], recv_x.at[d - 1], at_x(d)).start()
    remote(mine, mine, send_c.at[0], recv_c.at[0], sibling).start()
    for d in range(1, SIZE_X):
        other = ((x + SIZE_X - d) % SIZE_X) * 2 + core
        remote(result.at[other], result.at[other], send_x.at[d - 1], recv_x.at[d - 1], at_x(d)).wait_recv()
        remote(result.at[other], result.at[other], send_c.at[d], recv_c.at[d], sibling).start()
    for d in range(SIZE_X):
        other = ((x + SIZE_X - d) % SIZE_X) * 2 + 1 - core
        remote(result.at[other], result.at[other], send_c.at[d], recv_c.at[d], sibling).wait_recv()

    for i in range(BLOCKS):
        for j in range(i, BLOCKS):
            owner, place = block_place(i, j)
            whole[i * BLOCK : (i + 1) * BLOCK, j * BLOCK : (j + 1) * BLOCK] = result[owner, place * BLOCK : (place + 1) * BLOCK, :]

    cholesky(whole, work)
    out_ref[...] = whole[:, pl.ds(pl.multiple_of(b * BLOCK, BLOCK), BLOCK)]

    for d in range(1, SIZE_Y):
        remote(from_y.at[0], from_y.at[0], send_y.at[d - 1], recv_y.at[d - 1], at_y(d)).wait_send()
        remote(mine.at[pl.ds(0, PART_Y)], mine.at[pl.ds(0, PART_Y)], send_gy.at[d - 1], recv_gy.at[d - 1], at_y(d)).wait_send()
    for d in range(1, SIZE_Z):
        there = (z + d) % SIZE_Z

        @pl.when(there < OWNERS)
        def _():
            remote(from_z.at[0], from_z.at[0], send_z.at[d - 1], recv_z.at[d - 1], at_z(d)).wait_send()

        @pl.when(z < OWNERS)
        def _():
            remote(from_z.at[0], from_z.at[0], send_gz.at[d - 1], recv_gz.at[d - 1], at_z(d)).wait_send()

    for k in range(count):
        for copy in (*first_halo(k), *second_halo(k), to_left(k), to_right(k), on_left(k), on_right(k)):
            copy.wait_send()
        for slot in range(2):
            across(filtered, slot, k).wait_send()
        store(k).wait()
    for d in range(1, SIZE_X):
        remote(mine, mine, send_x.at[d - 1], recv_x.at[d - 1], at_x(d)).wait_send()
    for d in range(SIZE_X):
        remote(mine, mine, send_c.at[d], recv_c.at[d], sibling).wait_send()


def cholesky(S, work):
    row = lax.broadcasted_iota(jnp.int32, (BLOCK, BLOCK), 0)
    column = lax.broadcasted_iota(jnp.int32, (BLOCK, BLOCK), 1)

    def step(k, carry):
        for kk in range(BLOCKS):

            @pl.when(k == kk)
            def _():
                work[:, 0:BLOCK] = S[kk * BLOCK : (kk + 1) * BLOCK, kk * BLOCK : (kk + 1) * BLOCK]

        work[:, BLOCK:] = jnp.where(row == column, 1.0, 0.0)
        factor_diagonal(work)
        for kk in range(BLOCKS):

            @pl.when(k == kk)
            def _():
                lo, hi = kk * BLOCK, (kk + 1) * BLOCK
                S[lo:hi, lo:hi] = jnp.where(column >= row, work[:, 0:BLOCK], 0.0)
                if kk < BLOCKS - 1:
                    inverse = jnp.where(column <= row, work[:, BLOCK:], 0.0)
                    S[lo:hi, hi:] = jnp.dot(inverse, S[lo:hi, hi:], precision=HIGHEST, preferred_element_type=jnp.float32)
                    for a in range(kk + 1, BLOCKS):
                        left = S[lo:hi, a * BLOCK : (a + 1) * BLOCK]
                        S[a * BLOCK : (a + 1) * BLOCK, a * BLOCK :] -= lax.dot_general(
                            left, S[lo:hi, a * BLOCK :], (((0,), (0,)), ((), ())),
                            precision=HIGHEST, preferred_element_type=jnp.float32,
                        )

        return carry

    lax.fori_loop(0, BLOCKS, step, 0)
    for a in range(1, BLOCKS):
        S[a * BLOCK : (a + 1) * BLOCK, 0 : a * BLOCK] = jnp.zeros((BLOCK, a * BLOCK), jnp.float32)


def filtered_factor(orbitals, potential, cells):
    dma = pltpu.SemaphoreType.DMA
    field = pltpu.VMEM((2, GY, GX, BLOCK), jnp.float32)
    count = len(CHUNKS)
    return pl.pallas_call(
        functools.partial(factor_kernel, 1.0 / cells),
        out_shape=(
            jax.ShapeDtypeStruct((2, GY, GX, BLOCK), jnp.float32),
            jax.ShapeDtypeStruct((TOTAL, BLOCK), jnp.float32),
        ),
        in_specs=[pl.BlockSpec(memory_space=pl.ANY), pl.BlockSpec(memory_space=pltpu.VMEM)],
        out_specs=(pl.BlockSpec(memory_space=pl.ANY), pl.BlockSpec(memory_space=pltpu.VMEM)),
        scratch_shapes=[
            field, field, field, field, field, field, field, field,
            pltpu.VMEM((KEPT - 1, 2, GY, GX, BLOCK), jnp.float32),
            pltpu.VMEM((GY, GX, BLOCK), jnp.float32),
            pltpu.VMEM((ROWS, BLOCK), jnp.float32),
            pltpu.VMEM((SIZE_Y - 1, PART_Y, BLOCK), jnp.float32),
            pltpu.VMEM((SIZE_Z - 1, PART_Z, BLOCK), jnp.float32),
            pltpu.VMEM((PART_Y, BLOCK), jnp.float32),
            pltpu.VMEM((BLOCKS, ROWS, BLOCK), jnp.float32),
            pltpu.VMEM((TOTAL, TOTAL), jnp.float32),
            pltpu.VMEM((BLOCK, 2 * BLOCK), jnp.float32),
            dma((1 + count,)),
            dma((2, count)), dma((2, count)),
            dma((2, count)), dma((2, count)),
            dma((4, count)), dma((4, count)),
            dma((2, count)), dma((2, count)),
            dma((SIZE_Y - 1,)), dma((SIZE_Y - 1,)),
            dma((SIZE_Z - 1,)), dma((SIZE_Z - 1,)),
            dma((SIZE_Z - 1,)), dma((SIZE_Z - 1,)),
            dma((SIZE_Y - 1,)), dma((SIZE_Y - 1,)),
            dma((SIZE_X - 1,)), dma((SIZE_X - 1,)),
            dma((SIZE_X,)), dma((SIZE_X,)),
        ],
        compiler_params=pltpu.CompilerParams(
            collective_id=1, has_side_effects=True, vmem_limit_bytes=48 * 1024 * 1024
        ),
        name="filtered_factor",
    )(orbitals, potential)


def local(orbitals, potential):
    cells = orbitals.shape[0] * GY * GX * SIZE_Y * SIZE_Z
    return filtered_factor(orbitals, potential.reshape(-1, GX).T, cells)


def solution(mesh):
    placed = (P("grid", None, None, "orb"), P("grid", None))
    return jax.shard_map(
        local,
        mesh=mesh,
        in_specs=placed,
        out_specs=(P("grid", None, None, "orb"), P(None, "orb")),
        check_vma=False,
    )
```

```python
import functools

import jax
import jax.numpy as jnp
from jax import lax
from jax.experimental import pallas as pl
from jax.experimental.pallas import tpu as pltpu
from jax.sharding import PartitionSpec as P

GX = 32
GY = 32
LOWER = 1.0
UPPER = 10.0
KINETIC = 0.5
CENTRE = 0.5 * (UPPER + LOWER)
HALF_WIDTH = 0.5 * (UPPER - LOWER)

SIZE_X = 4
SIZE_Y = 4
SIZE_Z = 16
BLOCK = 128
BLOCKS = 8
KEPT = 5
ROWS = KEPT * BLOCK
PART_Y = ROWS // SIZE_Y
PART_Z = 16
OWNERS = PART_Y // PART_Z
GROUP = 4
TOTAL = BLOCK * BLOCKS

CHUNKS = tuple((4 * i, 4) for i in range(7)) + ((28, 2), (30, 2))
AHEAD = 2

MESH = pl.DeviceIdType.MESH
HIGHEST = lax.Precision.HIGHEST


def factor_diagonal(work):
    sub = lax.broadcasted_iota(jnp.int32, (8, 128), 0)
    for p in range(16):
        o = 8 * p
        pl_ = work[o:o+8, 0:128]
        pr_ = work[o:o+8, 128:256]
        s = {}
        for j in range(8):
            column = jnp.broadcast_to(pl_[:, o+j:o+j+1], (8, 128))
            for i in range(j + 1):
                s[i, j] = jnp.broadcast_to(column[i:i+1, :], (8, 128))
        r = [None]*8
        u = {}
        rows_l, rows_r = [], []
        L, R = pl_, pr_
        for k in range(8):
            r[k] = lax.rsqrt(s[k, k])
            for j in range(k+1, 8):
                u[k, j] = s[k, j] * r[k]
            for i in range(k+1, 8):
                for j in range(i, 8):
                    s[i, j] = s[i, j] - u[k, i] * u[k, j]
            kl = jnp.broadcast_to(L[k:k+1, :], (8, 128)) * r[k]
            kr = jnp.broadcast_to(R[k:k+1, :], (8, 128)) * r[k]
            rows_l.append(kl); rows_r.append(kr)
            if k < 7:
                col = u[k, 7]
                for i in range(6, k, -1):
                    col = jnp.where(sub == i, u[k, i], col)
                col = jnp.where(sub > k, col, 0.0)
                L = L - col * kl
                R = R - col * kr
        outl, outr = rows_l[7], rows_r[7]
        for k in range(6, -1, -1):
            outl = jnp.where(sub == k, rows_l[k], outl)
            outr = jnp.where(sub == k, rows_r[k], outr)
        work[o:o+8, 0:128] = outl
        work[o:o+8, 128:256] = outr
        for v in range(p+1, 16):
            a = 8 * v
            wl = work[a:a+8, 0:128]
            wr = work[a:a+8, 128:256]
            c = [jnp.broadcast_to(wl[:, o+k:o+k+1], (8, 128)) for k in range(8)]
            for k in range(8):
                c[k] = c[k] * r[k]
                for j in range(k+1, 8):
                    c[j] = c[j] - u[k, j] * c[k]
                wl = wl - c[k] * rows_l[k]
                wr = wr - c[k] * rows_r[k]
            work[a:a+8, 0:128] = wl
            work[a:a+8, 128:256] = wr


def block_place(row, column):
    if column - row < KEPT:
        return row, column - row
    return column, row - column + BLOCKS


def remote(src, dst, send, recv, device):
    return pltpu.make_async_remote_copy(
        src_ref=src, dst_ref=dst, send_sem=send, recv_sem=recv, device_id=device, device_id_type=MESH
    )


def add_slab(source, before, after, weight, y):
    rows = [source[layer, y] for layer in range(2)]
    scale = KINETIC / HALF_WIDTH
    out = []
    for layer in range(2):
        own = rows[layer]
        if layer == 0:
            near = rows[1] + before[1, y]
            far = before[0, y] + after[0, y]
        else:
            near = rows[0] + after[0, y]
            far = before[1, y] + after[1, y]
        near = near + (source[layer, (y + GY - 1) % GY] + source[layer, (y + 1) % GY])
        far = far + (source[layer, (y + GY - 2) % GY] + source[layer, (y + 2) % GY])
        near = near + (pltpu.roll(own, 1, 0) + pltpu.roll(own, GX - 1, 0))
        far = far + (pltpu.roll(own, 2, 0) + pltpu.roll(own, GX - 2, 0))
        out.append(weight[layer, y] * own - (4.0 / 3.0 * scale) * near + (1.0 / 12.0 * scale) * far)
    return out


def factor_kernel(
    scale, orbitals_ref, potential_ref, filtered_ref, out_ref,
    weight, slab, before, after, current, before_2, after_2, filtered, gathered, relay, part,
    from_y, from_z, summed, result, whole, work,
    local_sem, send_h, recv_h, send_k, recv_k, send_o, recv_o, send_s, recv_s,
    send_y, recv_y, send_z, recv_z, send_gz, recv_gz, send_gy, recv_gy, send_x, recv_x, send_c, recv_c,
):
    g, b = lax.axis_index("grid"), lax.axis_index("orb")
    y, z = g // SIZE_Z, g % SIZE_Z
    x, core = b // 2, b % 2
    slabs = SIZE_Y * SIZE_Z
    ahead, behind = ((g + 1) % slabs, b), ((g + slabs - 1) % slabs, b)
    count = len(CHUNKS)

    def at_y(d):
        return ((y + d) % SIZE_Y) * SIZE_Z + z, b

    def at_z(d):
        return y * SIZE_Z + (z + d) % SIZE_Z, b

    def at_x(d):
        return g, ((x + d) % SIZE_X) * 2 + core

    sibling = (g, x * 2 + 1 - core)

    barrier = pltpu.get_barrier_semaphore()
    for device in (ahead, behind):
        pl.semaphore_signal(barrier, inc=1, device_id=device, device_id_type=MESH)
    for d in range(1, SIZE_X):
        pl.semaphore_signal(barrier, inc=1, device_id=at_x(d), device_id_type=MESH)
    pl.semaphore_signal(barrier, inc=1, device_id=sibling, device_id_type=MESH)
    for d in range(1, SIZE_Y):
        pl.semaphore_signal(barrier, inc=1, device_id=at_y(d), device_id_type=MESH)
    for d in range(1, SIZE_Z):
        pl.semaphore_signal(barrier, inc=1, device_id=at_z(d), device_id_type=MESH)
    load = pltpu.make_async_copy(orbitals_ref, slab, local_sem.at[0])
    load.start()
    pl.semaphore_wait(barrier, SIZE_Y + SIZE_Z + SIZE_X)

    def rows(k):
        return pl.ds(CHUNKS[k][0], CHUNKS[k][1])

    def halo(source, low, high, send, recv, k):
        return (
            remote(source.at[:, rows(k)], low.at[:, rows(k)], send.at[0, k], recv.at[0, k], ahead),
            remote(source.at[:, rows(k)], high.at[:, rows(k)], send.at[1, k], recv.at[1, k], behind),
        )

    def first_halo(k):
        return halo(orbitals_ref, before, after, send_h, recv_h, k)

    def second_halo(k):
        return halo(current, before_2, after_2, send_k, recv_k, k)

    def to_left(k):
        return remote(filtered.at[:, rows(k)], gathered.at[1, :, rows(k)], send_o.at[0, k], recv_o.at[0, k], at_x(SIZE_X - 1))

    def to_right(k):
        return remote(filtered.at[1, rows(k)], relay.at[rows(k)], send_o.at[1, k], recv_o.at[1, k], at_x(1))

    def on_left(k):
        return remote(gathered.at[1, 0, rows(k)], gathered.at[3, 0, rows(k)], send_o.at[2, k], recv_o.at[2, k], at_x(SIZE_X - 1))

    def on_right(k):
        return remote(relay.at[rows(k)], gathered.at[3, 1, rows(k)], send_o.at[3, k], recv_o.at[3, k], at_x(1))

    def across(source, slot, k):
        return remote(source.at[:, rows(k)], gathered.at[2 * slot, :, rows(k)], send_s.at[slot, k], recv_s.at[slot, k], sibling)

    def store(k):
        return pltpu.make_async_copy(filtered.at[:, rows(k)], filtered_ref.at[:, rows(k)], local_sem.at[1 + k])

    for k in range(AHEAD):
        for copy in first_halo(k):
            copy.start()

    lines = BLOCK // GX
    for layer in range(2):
        for i in range(GY // lines):
            cells = potential_ref[layer : layer + 1, i * BLOCK : (i + 1) * BLOCK] + (7.5 * KINETIC - CENTRE)
            turned = jnp.broadcast_to(cells * (1.0 / HALF_WIDTH), (BLOCK, BLOCK)).T
            weight[layer, i * lines : (i + 1) * lines] = turned.reshape(lines, GX, BLOCK)
    part[...] = jnp.zeros_like(part)
    load.wait()

    def first_step(k):
        for copy in first_halo(k):
            copy.wait_recv()
        start, height = CHUNKS[k]

        def line(i, carry):
            for layer, value in enumerate(add_slab(slab, before, after, weight, start + i)):
                current[layer, start + i] = value
            return carry

        lax.fori_loop(0, height, line, 0)
        for copy in second_halo(k):
            copy.start()
        if k + AHEAD < count:
            for copy in first_halo(k + AHEAD):
                copy.start()

    def second_step(k):
        for copy in second_halo(k):
            copy.wait_recv()
        start, height = CHUNKS[k]

        def line(i, carry):
            for layer, value in enumerate(add_slab(current, before_2, after_2, weight, start + i)):
                filtered[layer, start + i] = 2.0 * value - slab[layer, start + i]
            return carry

        lax.fori_loop(0, height, line, 0)
        to_left(k).start()
        to_right(k).start()

        @pl.when(core == 1)
        def _():
            across(filtered, 0, k).start()

        store(k).start()

    def pass_on(k):
        to_left(k).wait_recv()
        on_left(k).start()
        to_right(k).wait_recv()
        on_right(k).start()

        @pl.when(core == 1)
        def _():
            across(gathered.at[1], 1, k).start()

        @pl.when(core == 0)
        def _():
            across(gathered.at[1], 0, k).start()

    def share(k):
        on_left(k).wait_recv()
        on_right(k).wait_recv()

        @pl.when(core == 0)
        def _():
            across(gathered.at[3], 1, k).start()

    def multiply(k):
        across(filtered, 0, k).wait_recv()
        across(filtered, 1, k).wait_recv()
        cells = 2 * CHUNKS[k][1] * GX
        own = filtered[:, rows(k)].reshape(cells, BLOCK)
        others = [own] + [gathered[j, :, rows(k)].reshape(cells, BLOCK) for j in range(KEPT - 1)]
        product = lax.dot_general(
            own, jnp.concatenate(others, axis=1), (((0,), (0,)), ((), ())),
            precision=HIGHEST, preferred_element_type=jnp.float32,
        )
        for j in range(KEPT):
            part[j * BLOCK : (j + 1) * BLOCK, :] += product[:, j * BLOCK : (j + 1) * BLOCK]

    stages = (second_step, pass_on, share, multiply)
    order = []

    def advance(k):
        order.append(k)
        for lag, stage in enumerate(stages):
            place = len(order) - 1 - lag
            if 0 <= place < count and order[place] is not None:
                stage(order[place])

    for k in range(count):
        first_step(k)
        if k - AHEAD >= 1:
            advance(k - AHEAD)
    advance(0)
    for k in range(count - AHEAD, count):
        advance(k)
    for lag in range(1, len(stages)):
        advance(None)

    for j in range(1, KEPT):

        @pl.when(b + j >= BLOCKS)
        def _():
            part[j * BLOCK : (j + 1) * BLOCK, :] = part[j * BLOCK : (j + 1) * BLOCK, :].T

    copies = []
    for d in range(1, SIZE_Y):
        there = (y + d) % SIZE_Y
        copies.append(remote(part.at[pl.ds(there * PART_Y, PART_Y)], from_y.at[d - 1], send_y.at[d - 1], recv_y.at[d - 1], at_y(d)))
        copies[-1].start()
    for c in copies:
        c.wait_recv()
    summed[...] = part[pl.ds(y * PART_Y, PART_Y), :] + from_y[0] + from_y[1] + from_y[2]

    for d in sorted(range(1, SIZE_Z), key=lambda d: -min(d, SIZE_Z - d)):
        there = (z + d) % SIZE_Z

        @pl.when(there < OWNERS)
        def _():
            remote(summed.at[pl.ds(there * PART_Z, PART_Z)], from_z.at[d - 1], send_z.at[d - 1], recv_z.at[d - 1], at_z(d)).start()

    def piece(source):
        return result.at[x, core, y, source // GROUP, source // 2 % 2, source % 2]

    def far(source, d):
        return remote(piece(source), piece(source), send_gz.at[0, d - 1], recv_gz.at[0, d - 1], at_z(GROUP * d))

    def near(member, d, full):
        place = (z + d) % GROUP - z % GROUP
        pieces = result.at[x, core, y, :, 0, member % 2] if full else result.at[x, core, y, 0:2, 1, member % 2]
        return remote(pieces, pieces, send_gz.at[1, d - 1], recv_gz.at[1, d - 1], (g + place, b))

    @pl.when(z < OWNERS)
    def _():
        for d in range(1, SIZE_Z):
            remote(summed.at[pl.ds(0, PART_Z)], from_z.at[d - 1], send_z.at[d - 1], recv_z.at[d - 1], at_z(d)).wait_recv()
        total = summed[pl.ds(z * PART_Z, PART_Z), :]
        for d in range(1, SIZE_Z):
            total = total + from_z[d - 1]
        result[x, core, y, z // GROUP, z // 2 % 2, z % 2] = total * scale
        for d in (2, 1, 3):
            far(z, d).start()

    for d in range(1, SIZE_Z // GROUP):
        source = (z + SIZE_Z - GROUP * d) % SIZE_Z

        @pl.when(source < OWNERS)
        def _():
            far(source, d).wait_recv()

    for full in (True, False):

        @pl.when((z % GROUP < 2) == full)
        def _():
            for d in (2, 1, 3):
                near(z % GROUP, d, full).start()

    for d in range(1, GROUP):
        member = (z + GROUP - d) % GROUP
        for full in (True, False):

            @pl.when((member < 2) == full)
            def _():
                near(member, d, full).wait_recv()

    def first_x(d, source):
        ref = result.at[source, core, y, :, 0]
        return remote(ref, ref, send_x.at[0, d - 1], recv_x.at[0, d - 1], at_x(d))

    def first_y(d, source):
        ref = result.at[x, core, source, 0:2, 1]
        return remote(ref, ref, send_gy.at[0, d - 1], recv_gy.at[0, d - 1], at_y(d))

    def then_y(d, source):
        ref = result.at[:, core, source, :, 0]
        return remote(ref, ref, send_gy.at[1, d - 1], recv_gy.at[1, d - 1], at_y(d))

    def then_x(d, source):
        ref = result.at[source, core, :, 0:2, 1]
        return remote(ref, ref, send_x.at[1, d - 1], recv_x.at[1, d - 1], at_x(d))

    def share_y(d, owner):
        ref = result.at[:, owner, (y + SIZE_Y - d) % SIZE_Y, :, 0]
        return remote(ref, ref, send_c.at[0, d], recv_c.at[0, d], sibling)

    def share_x(d, owner):
        ref = result.at[(x + SIZE_X - d) % SIZE_X, owner, :, 0:2, 1]
        return remote(ref, ref, send_c.at[1, d], recv_c.at[1, d], sibling)

    def before_x(d):
        return (x + SIZE_X - d) % SIZE_X

    def before_y(d):
        return (y + SIZE_Y - d) % SIZE_Y

    for d in (2, 1, 3):
        first_x(d, x).start()
        first_y(d, y).start()
    for d in range(1, SIZE_X):
        first_x(d, before_x(d)).wait_recv()
    for d in (2, 1, 3):
        then_y(d, y).start()
    share_y(0, core).start()
    for d in range(1, SIZE_Y):
        first_y(d, before_y(d)).wait_recv()
    for d in (2, 1, 3):
        then_x(d, x).start()
    share_x(0, core).start()
    for d in (1, 3, 2):
        then_y(d, before_y(d)).wait_recv()
        share_y(d, core).start()
        then_x(d, before_x(d)).wait_recv()
        share_x(d, core).start()
    for d in (0, 1, 3, 2):
        share_y(d, 1 - core).wait_recv()
        share_x(d, 1 - core).wait_recv()

    for i in range(BLOCKS):
        for j in range(i, BLOCKS):
            owner, place = block_place(i, j)
            for row in range(0, BLOCK, PART_Z):
                quarter, number = divmod((place * BLOCK + row) // PART_Z, OWNERS)
                whole[i * BLOCK + row : i * BLOCK + row + PART_Z, j * BLOCK : (j + 1) * BLOCK] = result[
                    owner // 2, owner % 2, quarter, number // GROUP, number // 2 % 2, number % 2
                ]

    cholesky(whole, work)
    out_ref[...] = whole[:, pl.ds(pl.multiple_of(b * BLOCK, BLOCK), BLOCK)]

    for d in range(1, SIZE_Y):
        remote(from_y.at[0], from_y.at[0], send_y.at[d - 1], recv_y.at[d - 1], at_y(d)).wait_send()
        first_y(d, y).wait_send()
        then_y(d, y).wait_send()
    for d in range(1, SIZE_X):
        first_x(d, x).wait_send()
        then_x(d, x).wait_send()
    for d in range(SIZE_X):
        share_y(d, core).wait_send()
        share_x(d, core).wait_send()
    for d in range(1, SIZE_Z):
        there = (z + d) % SIZE_Z

        @pl.when(there < OWNERS)
        def _():
            remote(from_z.at[0], from_z.at[0], send_z.at[d - 1], recv_z.at[d - 1], at_z(d)).wait_send()

    @pl.when(z < OWNERS)
    def _():
        for d in range(1, SIZE_Z // GROUP):
            far(z, d).wait_send()

    for full in (True, False):

        @pl.when((z % GROUP < 2) == full)
        def _():
            for d in range(1, GROUP):
                near(z % GROUP, d, full).wait_send()

    for k in range(count):
        for copy in (*first_halo(k), *second_halo(k), to_left(k), to_right(k), on_left(k), on_right(k)):
            copy.wait_send()
        for slot in range(2):
            across(filtered, slot, k).wait_send()
        store(k).wait()


def cholesky(S, work):
    row = lax.broadcasted_iota(jnp.int32, (BLOCK, BLOCK), 0)
    column = lax.broadcasted_iota(jnp.int32, (BLOCK, BLOCK), 1)

    def step(k, carry):
        for kk in range(BLOCKS):

            @pl.when(k == kk)
            def _():
                work[:, 0:BLOCK] = S[kk * BLOCK : (kk + 1) * BLOCK, kk * BLOCK : (kk + 1) * BLOCK]

        work[:, BLOCK:] = jnp.where(row == column, 1.0, 0.0)
        factor_diagonal(work)
        for kk in range(BLOCKS):

            @pl.when(k == kk)
            def _():
                lo, hi = kk * BLOCK, (kk + 1) * BLOCK
                S[lo:hi, lo:hi] = jnp.where(column >= row, work[:, 0:BLOCK], 0.0)
                if kk < BLOCKS - 1:
                    inverse = jnp.where(column <= row, work[:, BLOCK:], 0.0)
                    S[lo:hi, hi:] = jnp.dot(inverse, S[lo:hi, hi:], precision=HIGHEST, preferred_element_type=jnp.float32)
                    for a in range(kk + 1, BLOCKS):
                        left = S[lo:hi, a * BLOCK : (a + 1) * BLOCK]
                        S[a * BLOCK : (a + 1) * BLOCK, a * BLOCK :] -= lax.dot_general(
                            left, S[lo:hi, a * BLOCK :], (((0,), (0,)), ((), ())),
                            precision=HIGHEST, preferred_element_type=jnp.float32,
                        )

        return carry

    lax.fori_loop(0, BLOCKS, step, 0)
    for a in range(1, BLOCKS):
        S[a * BLOCK : (a + 1) * BLOCK, 0 : a * BLOCK] = jnp.zeros((BLOCK, a * BLOCK), jnp.float32)


def filtered_factor(orbitals, potential, cells):
    dma = pltpu.SemaphoreType.DMA
    field = pltpu.VMEM((2, GY, GX, BLOCK), jnp.float32)
    count = len(CHUNKS)
    return pl.pallas_call(
        functools.partial(factor_kernel, 1.0 / cells),
        out_shape=(
            jax.ShapeDtypeStruct((2, GY, GX, BLOCK), jnp.float32),
            jax.ShapeDtypeStruct((TOTAL, BLOCK), jnp.float32),
        ),
        in_specs=[pl.BlockSpec(memory_space=pl.ANY), pl.BlockSpec(memory_space=pltpu.VMEM)],
        out_specs=(pl.BlockSpec(memory_space=pl.ANY), pl.BlockSpec(memory_space=pltpu.VMEM)),
        scratch_shapes=[
            field, field, field, field, field, field, field, field,
            pltpu.VMEM((KEPT - 1, 2, GY, GX, BLOCK), jnp.float32),
            pltpu.VMEM((GY, GX, BLOCK), jnp.float32),
            pltpu.VMEM((ROWS, BLOCK), jnp.float32),
            pltpu.VMEM((SIZE_Y - 1, PART_Y, BLOCK), jnp.float32),
            pltpu.VMEM((SIZE_Z - 1, PART_Z, BLOCK), jnp.float32),
            pltpu.VMEM((PART_Y, BLOCK), jnp.float32),
            pltpu.VMEM((SIZE_X, 2, SIZE_Y, 3, 2, 2, PART_Z, BLOCK), jnp.float32),
            pltpu.VMEM((TOTAL, TOTAL), jnp.float32),
            pltpu.VMEM((BLOCK, 2 * BLOCK), jnp.float32),
            dma((1 + count,)),
            dma((2, count)), dma((2, count)),
            dma((2, count)), dma((2, count)),
            dma((4, count)), dma((4, count)),
            dma((2, count)), dma((2, count)),
            dma((SIZE_Y - 1,)), dma((SIZE_Y - 1,)),
            dma((SIZE_Z - 1,)), dma((SIZE_Z - 1,)),
            dma((2, GROUP - 1)), dma((2, GROUP - 1)),
            dma((2, SIZE_Y - 1)), dma((2, SIZE_Y - 1)),
            dma((2, SIZE_X - 1)), dma((2, SIZE_X - 1)),
            dma((2, SIZE_X)), dma((2, SIZE_X)),
        ],
        compiler_params=pltpu.CompilerParams(
            collective_id=1, has_side_effects=True, vmem_limit_bytes=60 * 1024 * 1024
        ),
        name="filtered_factor",
    )(orbitals, potential)


def local(orbitals, potential):
    cells = orbitals.shape[0] * GY * GX * SIZE_Y * SIZE_Z
    return filtered_factor(orbitals, potential, cells)


def solution(mesh):
    placed = (P("grid", None, None, "orb"), P("grid", None))
    return jax.shard_map(
        local,
        mesh=mesh,
        in_specs=placed,
        out_specs=(P("grid", None, None, "orb"), P(None, "orb")),
        check_vma=False,
    )
```

```python
import functools

import jax
import jax.numpy as jnp
from jax import lax
from jax.experimental import pallas as pl
from jax.experimental.pallas import tpu as pltpu
from jax.sharding import PartitionSpec as P

GX = 32
GY = 32
LOWER = 1.0
UPPER = 10.0
KINETIC = 0.5
CENTRE = 0.5 * (UPPER + LOWER)
HALF_WIDTH = 0.5 * (UPPER - LOWER)

SIZE_X = 4
SIZE_Y = 4
SIZE_Z = 16
BLOCK = 128
BLOCKS = 8
KEPT = 5
ROWS = KEPT * BLOCK
PART_Y = ROWS // SIZE_Y
PART_Z = 16
OWNERS = PART_Y // PART_Z
GROUP = 4
TOTAL = BLOCK * BLOCKS

CHUNKS = tuple((2 * i, 2) for i in range(16))
AHEAD = 4
LAGS = (0, 2, 4, 6)

MESH = pl.DeviceIdType.MESH
HIGHEST = lax.Precision.HIGHEST


def factor_diagonal(work):
    sub = lax.broadcasted_iota(jnp.int32, (8, 128), 0)
    for p in range(16):
        o = 8 * p
        pl_ = work[o:o+8, 0:128]
        pr_ = work[o:o+8, 128:256]
        s = {}
        for j in range(8):
            column = jnp.broadcast_to(pl_[:, o+j:o+j+1], (8, 128))
            for i in range(j + 1):
                s[i, j] = jnp.broadcast_to(column[i:i+1, :], (8, 128))
        r = [None]*8
        u = {}
        rows_l, rows_r = [], []
        L, R = pl_, pr_
        for k in range(8):
            r[k] = lax.rsqrt(s[k, k])
            for j in range(k+1, 8):
                u[k, j] = s[k, j] * r[k]
            for i in range(k+1, 8):
                for j in range(i, 8):
                    s[i, j] = s[i, j] - u[k, i] * u[k, j]
            kl = jnp.broadcast_to(L[k:k+1, :], (8, 128)) * r[k]
            kr = jnp.broadcast_to(R[k:k+1, :], (8, 128)) * r[k]
            rows_l.append(kl); rows_r.append(kr)
            if k < 7:
                col = u[k, 7]
                for i in range(6, k, -1):
                    col = jnp.where(sub == i, u[k, i], col)
                col = jnp.where(sub > k, col, 0.0)
                L = L - col * kl
                R = R - col * kr
        outl, outr = rows_l[7], rows_r[7]
        for k in range(6, -1, -1):
            outl = jnp.where(sub == k, rows_l[k], outl)
            outr = jnp.where(sub == k, rows_r[k], outr)
        work[o:o+8, 0:128] = outl
        work[o:o+8, 128:256] = outr
        for v in range(p+1, 16):
            a = 8 * v
            wl = work[a:a+8, 0:128]
            wr = work[a:a+8, 128:256]
            c = [jnp.broadcast_to(wl[:, o+k:o+k+1], (8, 128)) for k in range(8)]
            for k in range(8):
                c[k] = c[k] * r[k]
                for j in range(k+1, 8):
                    c[j] = c[j] - u[k, j] * c[k]
                wl = wl - c[k] * rows_l[k]
                wr = wr - c[k] * rows_r[k]
            work[a:a+8, 0:128] = wl
            work[a:a+8, 128:256] = wr


def block_place(row, column):
    if column - row < KEPT:
        return row, column - row
    return column, row - column + BLOCKS


def remote(src, dst, send, recv, device):
    return pltpu.make_async_remote_copy(
        src_ref=src, dst_ref=dst, send_sem=send, recv_sem=recv, device_id=device, device_id_type=MESH
    )


def add_slab(source, before, after, weight, y):
    rows = [source[layer, y] for layer in range(2)]
    scale = KINETIC / HALF_WIDTH
    out = []
    for layer in range(2):
        own = rows[layer]
        if layer == 0:
            near = rows[1] + before[1, y]
            far = before[0, y] + after[0, y]
        else:
            near = rows[0] + after[0, y]
            far = before[1, y] + after[1, y]
        near = near + (source[layer, (y + GY - 1) % GY] + source[layer, (y + 1) % GY])
        far = far + (source[layer, (y + GY - 2) % GY] + source[layer, (y + 2) % GY])
        near = near + (pltpu.roll(own, 1, 0) + pltpu.roll(own, GX - 1, 0))
        far = far + (pltpu.roll(own, 2, 0) + pltpu.roll(own, GX - 2, 0))
        out.append(weight[layer, y] * own - (4.0 / 3.0 * scale) * near + (1.0 / 12.0 * scale) * far)
    return out


def factor_kernel(
    scale, orbitals_ref, potential_ref, filtered, out_ref,
    weight, slab, before, after, current, before_2, after_2, gathered, relay, part,
    from_y, from_z, summed, result, whole, work,
    local_sem, send_h, recv_h, send_k, recv_k, send_o, recv_o, send_s, recv_s,
    send_y, recv_y, send_z, recv_z, send_gz, recv_gz, send_gy, recv_gy, send_x, recv_x, send_c, recv_c,
):
    g, b = lax.axis_index("grid"), lax.axis_index("orb")
    y, z = g // SIZE_Z, g % SIZE_Z
    x, core = b // 2, b % 2
    slabs = SIZE_Y * SIZE_Z
    ahead, behind = ((g + 1) % slabs, b), ((g + slabs - 1) % slabs, b)
    count = len(CHUNKS)

    def at_y(d):
        return ((y + d) % SIZE_Y) * SIZE_Z + z, b

    def at_z(d):
        return y * SIZE_Z + (z + d) % SIZE_Z, b

    def at_x(d):
        return g, ((x + d) % SIZE_X) * 2 + core

    sibling = (g, x * 2 + 1 - core)

    barrier = pltpu.get_barrier_semaphore()
    for device in (ahead, behind):
        pl.semaphore_signal(barrier, inc=1, device_id=device, device_id_type=MESH)
    for d in range(1, SIZE_X):
        pl.semaphore_signal(barrier, inc=1, device_id=at_x(d), device_id_type=MESH)
    pl.semaphore_signal(barrier, inc=1, device_id=sibling, device_id_type=MESH)
    for d in range(1, SIZE_Y):
        pl.semaphore_signal(barrier, inc=1, device_id=at_y(d), device_id_type=MESH)
    for d in range(1, SIZE_Z):
        pl.semaphore_signal(barrier, inc=1, device_id=at_z(d), device_id_type=MESH)
    load = pltpu.make_async_copy(orbitals_ref, slab, local_sem.at[0])
    load.start()
    pl.semaphore_wait(barrier, SIZE_Y + SIZE_Z + SIZE_X)

    def rows(k):
        return pl.ds(CHUNKS[k][0], CHUNKS[k][1])

    def halo(source, low, high, send, recv, k):
        return (
            remote(source.at[:, rows(k)], low.at[:, rows(k)], send.at[0, k], recv.at[0, k], ahead),
            remote(source.at[:, rows(k)], high.at[:, rows(k)], send.at[1, k], recv.at[1, k], behind),
        )

    def first_halo(k):
        return halo(orbitals_ref, before, after, send_h, recv_h, k)

    def second_halo(k):
        return halo(current, before_2, after_2, send_k, recv_k, k)

    def to_left(k):
        return remote(filtered.at[:, rows(k)], gathered.at[1, :, rows(k)], send_o.at[0, k], recv_o.at[0, k], at_x(SIZE_X - 1))

    def to_right(k):
        return remote(filtered.at[1, rows(k)], relay.at[rows(k)], send_o.at[1, k], recv_o.at[1, k], at_x(1))

    def on_left(k):
        return remote(gathered.at[1, 0, rows(k)], gathered.at[3, 0, rows(k)], send_o.at[2, k], recv_o.at[2, k], at_x(SIZE_X - 1))

    def on_right(k):
        return remote(relay.at[rows(k)], gathered.at[3, 1, rows(k)], send_o.at[3, k], recv_o.at[3, k], at_x(1))

    def across(source, slot, k):
        return remote(source.at[:, rows(k)], gathered.at[2 * slot, :, rows(k)], send_s.at[slot, k], recv_s.at[slot, k], sibling)

    for k in range(AHEAD):
        for copy in first_halo(k):
            copy.start()

    lines = BLOCK // GX
    for layer in range(2):
        for i in range(GY // lines):
            cells = potential_ref[layer : layer + 1, i * BLOCK : (i + 1) * BLOCK] + (7.5 * KINETIC - CENTRE)
            turned = jnp.broadcast_to(cells * (1.0 / HALF_WIDTH), (BLOCK, BLOCK)).T
            weight[layer, i * lines : (i + 1) * lines] = turned.reshape(lines, GX, BLOCK)
    part[...] = jnp.zeros_like(part)
    load.wait()

    def first_step(k):
        for copy in first_halo(k):
            copy.wait_recv()
        start, height = CHUNKS[k]

        def line(i, carry):
            for layer, value in enumerate(add_slab(slab, before, after, weight, start + i)):
                current[layer, start + i] = value
            return carry

        lax.fori_loop(0, height, line, 0)
        for copy in second_halo(k):
            copy.start()
        if k + AHEAD < count:
            for copy in first_halo(k + AHEAD):
                copy.start()

    def second_step(k):
        for copy in second_halo(k):
            copy.wait_recv()
        start, height = CHUNKS[k]

        def line(i, carry):
            for layer, value in enumerate(add_slab(current, before_2, after_2, weight, start + i)):
                filtered[layer, start + i] = 2.0 * value - slab[layer, start + i]
            return carry

        lax.fori_loop(0, height, line, 0)
        to_left(k).start()
        to_right(k).start()

        @pl.when(core == 1)
        def _():
            across(filtered, 0, k).start()


    def pass_on(k):
        to_left(k).wait_recv()
        on_left(k).start()
        to_right(k).wait_recv()
        on_right(k).start()

        @pl.when(core == 1)
        def _():
            across(gathered.at[1], 1, k).start()

        @pl.when(core == 0)
        def _():
            across(gathered.at[1], 0, k).start()

    def share(k):
        on_left(k).wait_recv()
        on_right(k).wait_recv()

        @pl.when(core == 0)
        def _():
            across(gathered.at[3], 1, k).start()

    def multiply(k):
        across(filtered, 0, k).wait_recv()
        across(filtered, 1, k).wait_recv()
        cells = 2 * CHUNKS[k][1] * GX
        own = filtered[:, rows(k)].reshape(cells, BLOCK)
        others = [own] + [gathered[j, :, rows(k)].reshape(cells, BLOCK) for j in range(KEPT - 1)]
        product = lax.dot_general(
            own, jnp.concatenate(others, axis=1), (((0,), (0,)), ((), ())),
            precision=HIGHEST, preferred_element_type=jnp.float32,
        )
        for j in range(KEPT):
            part[j * BLOCK : (j + 1) * BLOCK, :] += product[:, j * BLOCK : (j + 1) * BLOCK]

    stages = (second_step, pass_on, share, multiply)
    order = []

    def advance(k):
        order.append(k)
        for lag, stage in zip(LAGS, stages):
            place = len(order) - 1 - lag
            if 0 <= place < count and order[place] is not None:
                stage(order[place])

    for k in range(count):
        first_step(k)
        if k - AHEAD >= 1:
            advance(k - AHEAD)
    advance(0)
    for k in range(count - AHEAD, count):
        advance(k)
    for _ in range(LAGS[-1]):
        advance(None)

    for j in range(1, KEPT):

        @pl.when(b + j >= BLOCKS)
        def _():
            part[j * BLOCK : (j + 1) * BLOCK, :] = part[j * BLOCK : (j + 1) * BLOCK, :].T

    copies = []
    for d in range(1, SIZE_Y):
        there = (y + d) % SIZE_Y
        copies.append(remote(part.at[pl.ds(there * PART_Y, PART_Y)], from_y.at[d - 1], send_y.at[d - 1], recv_y.at[d - 1], at_y(d)))
        copies[-1].start()
    for c in copies:
        c.wait_recv()
    summed[...] = part[pl.ds(y * PART_Y, PART_Y), :] + from_y[0] + from_y[1] + from_y[2]

    for d in sorted(range(1, SIZE_Z), key=lambda d: -min(d, SIZE_Z - d)):
        there = (z + d) % SIZE_Z

        @pl.when(there < OWNERS)
        def _():
            remote(summed.at[pl.ds(there * PART_Z, PART_Z)], from_z.at[d - 1], send_z.at[d - 1], recv_z.at[d - 1], at_z(d)).start()

    def piece(source):
        return result.at[x, core, y, source // GROUP, source // 2 % 2, source % 2]

    def far(source, d):
        return remote(piece(source), piece(source), send_gz.at[0, d - 1], recv_gz.at[0, d - 1], at_z(GROUP * d))

    def near(member, d, full):
        place = (z + d) % GROUP - z % GROUP
        pieces = result.at[x, core, y, :, 0, member % 2] if full else result.at[x, core, y, 0:2, 1, member % 2]
        return remote(pieces, pieces, send_gz.at[1, d - 1], recv_gz.at[1, d - 1], (g + place, b))

    @pl.when(z < OWNERS)
    def _():
        for d in range(1, SIZE_Z):
            remote(summed.at[pl.ds(0, PART_Z)], from_z.at[d - 1], send_z.at[d - 1], recv_z.at[d - 1], at_z(d)).wait_recv()
        total = summed[pl.ds(z * PART_Z, PART_Z), :]
        for d in range(1, SIZE_Z):
            total = total + from_z[d - 1]
        result[x, core, y, z // GROUP, z // 2 % 2, z % 2] = total * scale
        for d in (2, 1, 3):
            far(z, d).start()

    for d in range(1, SIZE_Z // GROUP):
        source = (z + SIZE_Z - GROUP * d) % SIZE_Z

        @pl.when(source < OWNERS)
        def _():
            far(source, d).wait_recv()

    for full in (True, False):

        @pl.when((z % GROUP < 2) == full)
        def _():
            for d in (2, 1, 3):
                near(z % GROUP, d, full).start()

    for d in range(1, GROUP):
        member = (z + GROUP - d) % GROUP
        for full in (True, False):

            @pl.when((member < 2) == full)
            def _():
                near(member, d, full).wait_recv()

    def first_x(d, source):
        ref = result.at[source, core, y, :, 0]
        return remote(ref, ref, send_x.at[0, d - 1], recv_x.at[0, d - 1], at_x(d))

    def first_y(d, source):
        ref = result.at[x, core, source, 0:2, 1]
        return remote(ref, ref, send_gy.at[0, d - 1], recv_gy.at[0, d - 1], at_y(d))

    def then_y(d, source):
        ref = result.at[:, core, source, :, 0]
        return remote(ref, ref, send_gy.at[1, d - 1], recv_gy.at[1, d - 1], at_y(d))

    def then_x(d, source):
        ref = result.at[source, core, :, 0:2, 1]
        return remote(ref, ref, send_x.at[1, d - 1], recv_x.at[1, d - 1], at_x(d))

    def share_y(d, owner):
        ref = result.at[:, owner, (y + SIZE_Y - d) % SIZE_Y, :, 0]
        return remote(ref, ref, send_c.at[0, d], recv_c.at[0, d], sibling)

    def share_x(d, owner):
        ref = result.at[(x + SIZE_X - d) % SIZE_X, owner, :, 0:2, 1]
        return remote(ref, ref, send_c.at[1, d], recv_c.at[1, d], sibling)

    def before_x(d):
        return (x + SIZE_X - d) % SIZE_X

    def before_y(d):
        return (y + SIZE_Y - d) % SIZE_Y

    for d in (2, 1, 3):
        first_x(d, x).start()
        first_y(d, y).start()
    for d in range(1, SIZE_X):
        first_x(d, before_x(d)).wait_recv()
    for d in (2, 1, 3):
        then_y(d, y).start()
    share_y(0, core).start()
    for d in range(1, SIZE_Y):
        first_y(d, before_y(d)).wait_recv()
    for d in (2, 1, 3):
        then_x(d, x).start()
    share_x(0, core).start()
    for d in (1, 3, 2):
        then_y(d, before_y(d)).wait_recv()
        share_y(d, core).start()
        then_x(d, before_x(d)).wait_recv()
        share_x(d, core).start()
    for d in (0, 1, 3, 2):
        share_y(d, 1 - core).wait_recv()
        share_x(d, 1 - core).wait_recv()

    for i in range(BLOCKS):
        for j in range(i, BLOCKS):
            owner, place = block_place(i, j)
            for row in range(0, BLOCK, PART_Z):
                quarter, number = divmod((place * BLOCK + row) // PART_Z, OWNERS)
                whole[i * BLOCK + row : i * BLOCK + row + PART_Z, j * BLOCK : (j + 1) * BLOCK] = result[
                    owner // 2, owner % 2, quarter, number // GROUP, number // 2 % 2, number % 2
                ]

    cholesky(whole, work)
    out_ref[...] = whole[:, pl.ds(pl.multiple_of(b * BLOCK, BLOCK), BLOCK)]

    for d in range(1, SIZE_Y):
        remote(from_y.at[0], from_y.at[0], send_y.at[d - 1], recv_y.at[d - 1], at_y(d)).wait_send()
        first_y(d, y).wait_send()
        then_y(d, y).wait_send()
    for d in range(1, SIZE_X):
        first_x(d, x).wait_send()
        then_x(d, x).wait_send()
    for d in range(SIZE_X):
        share_y(d, core).wait_send()
        share_x(d, core).wait_send()
    for d in range(1, SIZE_Z):
        there = (z + d) % SIZE_Z

        @pl.when(there < OWNERS)
        def _():
            remote(from_z.at[0], from_z.at[0], send_z.at[d - 1], recv_z.at[d - 1], at_z(d)).wait_send()

    @pl.when(z < OWNERS)
    def _():
        for d in range(1, SIZE_Z // GROUP):
            far(z, d).wait_send()

    for full in (True, False):

        @pl.when((z % GROUP < 2) == full)
        def _():
            for d in range(1, GROUP):
                near(z % GROUP, d, full).wait_send()

    for k in range(count):
        for copy in (*first_halo(k), *second_halo(k), to_left(k), to_right(k), on_left(k), on_right(k)):
            copy.wait_send()
        for slot in range(2):
            across(filtered, slot, k).wait_send()


def cholesky(S, work):
    row = lax.broadcasted_iota(jnp.int32, (BLOCK, BLOCK), 0)
    column = lax.broadcasted_iota(jnp.int32, (BLOCK, BLOCK), 1)

    def step(k, carry):
        for kk in range(BLOCKS):

            @pl.when(k == kk)
            def _():
                work[:, 0:BLOCK] = S[kk * BLOCK : (kk + 1) * BLOCK, kk * BLOCK : (kk + 1) * BLOCK]

        work[:, BLOCK:] = jnp.where(row == column, 1.0, 0.0)
        factor_diagonal(work)
        for kk in range(BLOCKS):

            @pl.when(k == kk)
            def _():
                lo, hi = kk * BLOCK, (kk + 1) * BLOCK
                S[lo:hi, lo:hi] = jnp.where(column >= row, work[:, 0:BLOCK], 0.0)
                if kk < BLOCKS - 1:
                    inverse = jnp.where(column <= row, work[:, BLOCK:], 0.0)
                    S[lo:hi, hi:] = jnp.dot(inverse, S[lo:hi, hi:], precision=HIGHEST, preferred_element_type=jnp.float32)
                    for a in range(kk + 1, BLOCKS):
                        left = S[lo:hi, a * BLOCK : (a + 1) * BLOCK]
                        S[a * BLOCK : (a + 1) * BLOCK, a * BLOCK :] -= lax.dot_general(
                            left, S[lo:hi, a * BLOCK :], (((0,), (0,)), ((), ())),
                            precision=HIGHEST, preferred_element_type=jnp.float32,
                        )

        return carry

    lax.fori_loop(0, BLOCKS, step, 0)
    for a in range(1, BLOCKS):
        S[a * BLOCK : (a + 1) * BLOCK, 0 : a * BLOCK] = jnp.zeros((BLOCK, a * BLOCK), jnp.float32)


def filtered_factor(orbitals, potential, cells):
    dma = pltpu.SemaphoreType.DMA
    field = pltpu.VMEM((2, GY, GX, BLOCK), jnp.float32)
    count = len(CHUNKS)
    return pl.pallas_call(
        functools.partial(factor_kernel, 1.0 / cells),
        out_shape=(
            jax.ShapeDtypeStruct((2, GY, GX, BLOCK), jnp.float32),
            jax.ShapeDtypeStruct((TOTAL, BLOCK), jnp.float32),
        ),
        in_specs=[pl.BlockSpec(memory_space=pltpu.HBM), pl.BlockSpec(memory_space=pltpu.VMEM)],
        out_specs=(pl.BlockSpec(memory_space=pltpu.VMEM), pl.BlockSpec(memory_space=pltpu.VMEM)),
        scratch_shapes=[
            field, field, field, field, field, field, field,
            pltpu.VMEM((KEPT - 1, 2, GY, GX, BLOCK), jnp.float32),
            pltpu.VMEM((GY, GX, BLOCK), jnp.float32),
            pltpu.VMEM((ROWS, BLOCK), jnp.float32),
            pltpu.VMEM((SIZE_Y - 1, PART_Y, BLOCK), jnp.float32),
            pltpu.VMEM((SIZE_Z - 1, PART_Z, BLOCK), jnp.float32),
            pltpu.VMEM((PART_Y, BLOCK), jnp.float32),
            pltpu.VMEM((SIZE_X, 2, SIZE_Y, 3, 2, 2, PART_Z, BLOCK), jnp.float32),
            pltpu.VMEM((TOTAL, TOTAL), jnp.float32),
            pltpu.VMEM((BLOCK, 2 * BLOCK), jnp.float32),
            dma((1,)),
            dma((2, count)), dma((2, count)),
            dma((2, count)), dma((2, count)),
            dma((4, count)), dma((4, count)),
            dma((2, count)), dma((2, count)),
            dma((SIZE_Y - 1,)), dma((SIZE_Y - 1,)),
            dma((SIZE_Z - 1,)), dma((SIZE_Z - 1,)),
            dma((2, GROUP - 1)), dma((2, GROUP - 1)),
            dma((2, SIZE_Y - 1)), dma((2, SIZE_Y - 1)),
            dma((2, SIZE_X - 1)), dma((2, SIZE_X - 1)),
            dma((2, SIZE_X)), dma((2, SIZE_X)),
        ],
        compiler_params=pltpu.CompilerParams(
            collective_id=1, has_side_effects=True, vmem_limit_bytes=40 * 1024 * 1024
        ),
        name="filtered_factor",
    )(orbitals, potential)


def local(orbitals, potential):
    cells = orbitals.shape[0] * GY * GX * SIZE_Y * SIZE_Z
    return filtered_factor(orbitals, potential, cells)


def solution(mesh):
    placed = (P("grid", None, None, "orb"), P("grid", None))
    return jax.shard_map(
        local,
        mesh=mesh,
        in_specs=placed,
        out_specs=(P("grid", None, None, "orb"), P(None, "orb")),
        check_vma=False,
    )
```

```python
import functools

import jax
import jax.numpy as jnp
from jax import lax
from jax.experimental import pallas as pl
from jax.experimental.pallas import tpu as pltpu
from jax.sharding import PartitionSpec as P

GX = 32
GY = 32
LOWER = 1.0
UPPER = 10.0
KINETIC = 0.5
CENTRE = 0.5 * (UPPER + LOWER)
HALF_WIDTH = 0.5 * (UPPER - LOWER)

SIZE_X = 4
SIZE_Y = 4
SIZE_Z = 16
BLOCK = 128
BLOCKS = 8
KEPT = 5
ROWS = KEPT * BLOCK
PART_Y = ROWS // SIZE_Y
PART_Z = 16
OWNERS = PART_Y // PART_Z
GROUP = 4
TOTAL = BLOCK * BLOCKS

CHUNKS = tuple((2 * i, 2) for i in range(16))
AHEAD = 4
LAGS = (0, 2, 4, 6)

MESH = pl.DeviceIdType.MESH
HIGHEST = lax.Precision.HIGHEST


def factor_diagonal(work):
    sub = lax.broadcasted_iota(jnp.int32, (8, 128), 0)
    for p in range(16):
        o = 8 * p
        pl_ = work[o:o+8, 0:128]
        pr_ = work[o:o+8, 128:256]
        s = {}
        for j in range(8):
            column = jnp.broadcast_to(pl_[:, o+j:o+j+1], (8, 128))
            for i in range(j + 1):
                s[i, j] = jnp.broadcast_to(column[i:i+1, :], (8, 128))
        r = [None]*8
        u = {}
        rows_l, rows_r = [], []
        L, R = pl_, pr_
        for k in range(8):
            r[k] = lax.rsqrt(s[k, k])
            for j in range(k+1, 8):
                u[k, j] = s[k, j] * r[k]
            for i in range(k+1, 8):
                for j in range(i, 8):
                    s[i, j] = s[i, j] - u[k, i] * u[k, j]
            kl = jnp.broadcast_to(L[k:k+1, :], (8, 128)) * r[k]
            kr = jnp.broadcast_to(R[k:k+1, :], (8, 128)) * r[k]
            rows_l.append(kl); rows_r.append(kr)
            if k < 7:
                col = u[k, 7]
                for i in range(6, k, -1):
                    col = jnp.where(sub == i, u[k, i], col)
                col = jnp.where(sub > k, col, 0.0)
                L = L - col * kl
                R = R - col * kr
        outl, outr = rows_l[7], rows_r[7]
        for k in range(6, -1, -1):
            outl = jnp.where(sub == k, rows_l[k], outl)
            outr = jnp.where(sub == k, rows_r[k], outr)
        work[o:o+8, 0:128] = outl
        work[o:o+8, 128:256] = outr
        for v in range(p+1, 16):
            a = 8 * v
            wl = work[a:a+8, 0:128]
            wr = work[a:a+8, 128:256]
            c = [jnp.broadcast_to(wl[:, o+k:o+k+1], (8, 128)) for k in range(8)]
            for k in range(8):
                c[k] = c[k] * r[k]
                for j in range(k+1, 8):
                    c[j] = c[j] - u[k, j] * c[k]
                wl = wl - c[k] * rows_l[k]
                wr = wr - c[k] * rows_r[k]
            work[a:a+8, 0:128] = wl
            work[a:a+8, 128:256] = wr


def block_place(row, column):
    if column - row < KEPT:
        return row, column - row
    return column, row - column + BLOCKS


def remote(src, dst, send, recv, device):
    return pltpu.make_async_remote_copy(
        src_ref=src, dst_ref=dst, send_sem=send, recv_sem=recv, device_id=device, device_id_type=MESH
    )


def add_slab(source, before, after, weight, y):
    rows = [source[layer, y] for layer in range(2)]
    scale = KINETIC / HALF_WIDTH
    out = []
    for layer in range(2):
        own = rows[layer]
        if layer == 0:
            near = rows[1] + before[1, y]
            far = before[0, y] + after[0, y]
        else:
            near = rows[0] + after[0, y]
            far = before[1, y] + after[1, y]
        near = near + (source[layer, (y + GY - 1) % GY] + source[layer, (y + 1) % GY])
        far = far + (source[layer, (y + GY - 2) % GY] + source[layer, (y + 2) % GY])
        near = near + (pltpu.roll(own, 1, 0) + pltpu.roll(own, GX - 1, 0))
        far = far + (pltpu.roll(own, 2, 0) + pltpu.roll(own, GX - 2, 0))
        out.append(weight[layer, y] * own - (4.0 / 3.0 * scale) * near + (1.0 / 12.0 * scale) * far)
    return out


def factor_kernel(
    scale, orbitals_ref, potential_ref, filtered, out_ref,
    weight, slab, before, after, current, before_2, after_2, gathered, relay, part,
    from_y, from_z, summed, result, whole, work, first,
    local_sem, send_h, recv_h, send_k, recv_k, send_o, recv_o, send_s, recv_s,
    send_y, recv_y, send_z, recv_z, send_gz, recv_gz, send_gy, recv_gy, send_x, recv_x, send_c, recv_c, send_e, recv_e,
):
    g, b = lax.axis_index("grid"), lax.axis_index("orb")
    y, z = g // SIZE_Z, g % SIZE_Z
    x, core = b // 2, b % 2
    slabs = SIZE_Y * SIZE_Z
    ahead, behind = ((g + 1) % slabs, b), ((g + slabs - 1) % slabs, b)
    count = len(CHUNKS)

    def at_y(d):
        return ((y + d) % SIZE_Y) * SIZE_Z + z, b

    def at_z(d):
        return y * SIZE_Z + (z + d) % SIZE_Z, b

    def at_x(d):
        return g, ((x + d) % SIZE_X) * 2 + core

    sibling = (g, x * 2 + 1 - core)

    barrier = pltpu.get_barrier_semaphore()
    for device in (ahead, behind):
        pl.semaphore_signal(barrier, inc=1, device_id=device, device_id_type=MESH)
    for d in range(1, SIZE_X):
        pl.semaphore_signal(barrier, inc=1, device_id=at_x(d), device_id_type=MESH)
    pl.semaphore_signal(barrier, inc=1, device_id=sibling, device_id_type=MESH)
    for d in range(1, SIZE_Y):
        pl.semaphore_signal(barrier, inc=1, device_id=at_y(d), device_id_type=MESH)
    for d in range(1, SIZE_Z):
        pl.semaphore_signal(barrier, inc=1, device_id=at_z(d), device_id_type=MESH)
    load = pltpu.make_async_copy(orbitals_ref, slab, local_sem.at[0])
    load.start()
    pl.semaphore_wait(barrier, SIZE_Y + SIZE_Z + SIZE_X)

    def rows(k):
        return pl.ds(CHUNKS[k][0], CHUNKS[k][1])

    def halo(source, low, high, send, recv, k):
        return (
            remote(source.at[:, rows(k)], low.at[:, rows(k)], send.at[0, k], recv.at[0, k], ahead),
            remote(source.at[:, rows(k)], high.at[:, rows(k)], send.at[1, k], recv.at[1, k], behind),
        )

    def first_halo(k):
        return halo(orbitals_ref, before, after, send_h, recv_h, k)

    def second_halo(k):
        return halo(current, before_2, after_2, send_k, recv_k, k)

    def to_left(k):
        return remote(filtered.at[:, rows(k)], gathered.at[1, :, rows(k)], send_o.at[0, k], recv_o.at[0, k], at_x(SIZE_X - 1))

    def to_right(k):
        return remote(filtered.at[1, rows(k)], relay.at[rows(k)], send_o.at[1, k], recv_o.at[1, k], at_x(1))

    def on_left(k):
        return remote(gathered.at[1, 0, rows(k)], gathered.at[3, 0, rows(k)], send_o.at[2, k], recv_o.at[2, k], at_x(SIZE_X - 1))

    def on_right(k):
        return remote(relay.at[rows(k)], gathered.at[3, 1, rows(k)], send_o.at[3, k], recv_o.at[3, k], at_x(1))

    def across(source, slot, k):
        return remote(source.at[:, rows(k)], gathered.at[2 * slot, :, rows(k)], send_s.at[slot, k], recv_s.at[slot, k], sibling)

    for k in range(AHEAD):
        for copy in first_halo(k):
            copy.start()

    lines = BLOCK // GX
    for layer in range(2):
        for i in range(GY // lines):
            cells = potential_ref[layer : layer + 1, i * BLOCK : (i + 1) * BLOCK] + (7.5 * KINETIC - CENTRE)
            turned = jnp.broadcast_to(cells * (1.0 / HALF_WIDTH), (BLOCK, BLOCK)).T
            weight[layer, i * lines : (i + 1) * lines] = turned.reshape(lines, GX, BLOCK)
    part[...] = jnp.zeros_like(part)
    load.wait()

    def first_step(k):
        for copy in first_halo(k):
            copy.wait_recv()
        start, height = CHUNKS[k]

        def line(i, carry):
            for layer, value in enumerate(add_slab(slab, before, after, weight, start + i)):
                current[layer, start + i] = value
            return carry

        lax.fori_loop(0, height, line, 0)
        for copy in second_halo(k):
            copy.start()
        if k + AHEAD < count:
            for copy in first_halo(k + AHEAD):
                copy.start()

    def second_step(k):
        for copy in second_halo(k):
            copy.wait_recv()
        start, height = CHUNKS[k]

        def line(i, carry):
            for layer, value in enumerate(add_slab(current, before_2, after_2, weight, start + i)):
                filtered[layer, start + i] = 2.0 * value - slab[layer, start + i]
            return carry

        lax.fori_loop(0, height, line, 0)
        to_left(k).start()
        to_right(k).start()

        @pl.when(core == 1)
        def _():
            across(filtered, 0, k).start()


    def pass_on(k):
        to_left(k).wait_recv()
        on_left(k).start()
        to_right(k).wait_recv()
        on_right(k).start()

        @pl.when(core == 1)
        def _():
            across(gathered.at[1], 1, k).start()

        @pl.when(core == 0)
        def _():
            across(gathered.at[1], 0, k).start()

    def share(k):
        on_left(k).wait_recv()
        on_right(k).wait_recv()

        @pl.when(core == 0)
        def _():
            across(gathered.at[3], 1, k).start()

    def multiply(k):
        across(filtered, 0, k).wait_recv()
        across(filtered, 1, k).wait_recv()
        cells = 2 * CHUNKS[k][1] * GX
        own = filtered[:, rows(k)].reshape(cells, BLOCK)
        others = [own] + [gathered[j, :, rows(k)].reshape(cells, BLOCK) for j in range(KEPT - 1)]
        product = lax.dot_general(
            own, jnp.concatenate(others, axis=1), (((0,), (0,)), ((), ())),
            precision=HIGHEST, preferred_element_type=jnp.float32,
        )
        for j in range(KEPT):
            part[j * BLOCK : (j + 1) * BLOCK, :] += product[:, j * BLOCK : (j + 1) * BLOCK]

    stages = (second_step, pass_on, share, multiply)
    order = []

    def advance(k):
        order.append(k)
        for lag, stage in zip(LAGS, stages):
            place = len(order) - 1 - lag
            if 0 <= place < count and order[place] is not None:
                stage(order[place])

    for k in range(count):
        first_step(k)
        if k - AHEAD >= 1:
            advance(k - AHEAD)
    advance(0)
    for k in range(count - AHEAD, count):
        advance(k)
    for _ in range(LAGS[-1]):
        advance(None)

    for j in range(1, KEPT):

        @pl.when(b + j >= BLOCKS)
        def _():
            part[j * BLOCK : (j + 1) * BLOCK, :] = part[j * BLOCK : (j + 1) * BLOCK, :].T

    copies = []
    for d in range(1, SIZE_Y):
        there = (y + d) % SIZE_Y
        copies.append(remote(part.at[pl.ds(there * PART_Y, PART_Y)], from_y.at[d - 1], send_y.at[d - 1], recv_y.at[d - 1], at_y(d)))
        copies[-1].start()
    for c in copies:
        c.wait_recv()
    summed[...] = part[pl.ds(y * PART_Y, PART_Y), :] + from_y[0] + from_y[1] + from_y[2]

    for d in sorted(range(1, SIZE_Z), key=lambda d: -min(d, SIZE_Z - d)):
        there = (z + d) % SIZE_Z

        @pl.when(there < OWNERS)
        def _():
            remote(summed.at[pl.ds(there * PART_Z, PART_Z)], from_z.at[d - 1], send_z.at[d - 1], recv_z.at[d - 1], at_z(d)).start()

    def piece(source):
        return result.at[x, core, y, source // GROUP, source // 2 % 2, source % 2]

    def far(source, d):
        return remote(piece(source), piece(source), send_gz.at[0, d - 1], recv_gz.at[0, d - 1], at_z(GROUP * d))

    def near(member, d, full):
        place = (z + d) % GROUP - z % GROUP
        pieces = result.at[x, core, y, :, 0, member % 2] if full else result.at[x, core, y, 0:2, 1, member % 2]
        return remote(pieces, pieces, send_gz.at[1, d - 1], recv_gz.at[1, d - 1], (g + place, b))

    @pl.when(z < OWNERS)
    def _():
        for d in range(1, SIZE_Z):
            remote(summed.at[pl.ds(0, PART_Z)], from_z.at[d - 1], send_z.at[d - 1], recv_z.at[d - 1], at_z(d)).wait_recv()
        total = summed[pl.ds(z * PART_Z, PART_Z), :]
        for d in range(1, SIZE_Z):
            total = total + from_z[d - 1]
        result[x, core, y, z // GROUP, z // 2 % 2, z % 2] = total * scale
        for d in (2, 1, 3):
            far(z, d).start()

    for d in range(1, SIZE_Z // GROUP):
        source = (z + SIZE_Z - GROUP * d) % SIZE_Z

        @pl.when(source < OWNERS)
        def _():
            far(source, d).wait_recv()

    for full in (True, False):

        @pl.when((z % GROUP < 2) == full)
        def _():
            for d in (2, 1, 3):
                near(z % GROUP, d, full).start()

    for d in range(1, GROUP):
        member = (z + GROUP - d) % GROUP
        for full in (True, False):

            @pl.when((member < 2) == full)
            def _():
                near(member, d, full).wait_recv()

    def first_x(d, source):
        ref = result.at[source, core, y, :, 0]
        return remote(ref, ref, send_x.at[0, d - 1], recv_x.at[0, d - 1], at_x(d))

    def first_y(d, source):
        ref = result.at[x, core, source, 0:2, 1]
        return remote(ref, ref, send_gy.at[0, d - 1], recv_gy.at[0, d - 1], at_y(d))

    def then_y(d, source):
        ref = result.at[:, core, source, :, 0]
        return remote(ref, ref, send_gy.at[1, d - 1], recv_gy.at[1, d - 1], at_y(d))

    def then_x(d, source):
        ref = result.at[source, core, :, 0:2, 1]
        return remote(ref, ref, send_x.at[1, d - 1], recv_x.at[1, d - 1], at_x(d))

    def share_y(d, owner):
        ref = result.at[:, owner, (y + SIZE_Y - d) % SIZE_Y, :, 0]
        return remote(ref, ref, send_c.at[0, d], recv_c.at[0, d], sibling)

    def share_x(d, owner):
        ref = result.at[(x + SIZE_X - d) % SIZE_X, owner, :, 0:2, 1]
        return remote(ref, ref, send_c.at[1, d], recv_c.at[1, d], sibling)

    def before_x(d):
        return (x + SIZE_X - d) % SIZE_X

    def before_y(d):
        return (y + SIZE_Y - d) % SIZE_Y

    def lead(phase, d, device):
        return remote(first, first, send_e.at[phase, d - 1], recv_e.at[phase, d - 1], device)

    @pl.when((b == 0) & (y == 0))
    def _():
        first[...] = result[0, 0, 0, 0:2]
        for d in (2, 1, 3):
            lead(0, d, at_y(d)).start()

    for d in (2, 1, 3):
        first_x(d, x).start()
        first_y(d, y).start()
    for d in range(1, SIZE_X):
        first_x(d, before_x(d)).wait_recv()
    for d in (2, 1, 3):
        then_y(d, y).start()
    share_y(0, core).start()
    for d in range(1, SIZE_Y):
        first_y(d, before_y(d)).wait_recv()
    for d in (2, 1, 3):
        then_x(d, x).start()
    share_x(0, core).start()
    for d in range(1, SIZE_Y):

        @pl.when((b == 0) & (y == d))
        def _():
            lead(0, d, at_y(d)).wait_recv()

    @pl.when(b == 0)
    def _():
        for d in (2, 1, 3):
            lead(1, d, at_x(d)).start()

    for d in range(1, SIZE_X):

        @pl.when((core == 0) & (x == d))
        def _():
            lead(1, d, at_x(d)).wait_recv()

    @pl.when(core == 0)
    def _():
        lead(2, 1, sibling).start()

    @pl.when(core == 1)
    def _():
        lead(2, 1, sibling).wait_recv()

    def finish():
        for d in (1, 3, 2):
            then_y(d, before_y(d)).wait_recv()
            share_y(d, core).start()
            then_x(d, before_x(d)).wait_recv()
            share_x(d, core).start()
        for d in (0, 1, 3, 2):
            share_y(d, 1 - core).wait_recv()
            share_x(d, 1 - core).wait_recv()

        for i in range(BLOCKS):
            for j in range(i, BLOCKS):
                owner, place = block_place(i, j)
                for row in range(0, BLOCK, PART_Z):
                    quarter, number = divmod((place * BLOCK + row) // PART_Z, OWNERS)
                    whole[i * BLOCK + row : i * BLOCK + row + PART_Z, j * BLOCK : (j + 1) * BLOCK] = result[
                        owner // 2, owner % 2, quarter, number // GROUP, number // 2 % 2, number % 2
                    ]

    cholesky(whole, work, first, finish)
    out_ref[...] = whole[:, pl.ds(pl.multiple_of(b * BLOCK, BLOCK), BLOCK)]

    for d in range(1, SIZE_Y):
        remote(from_y.at[0], from_y.at[0], send_y.at[d - 1], recv_y.at[d - 1], at_y(d)).wait_send()
        first_y(d, y).wait_send()
        then_y(d, y).wait_send()
    for d in range(1, SIZE_X):
        first_x(d, x).wait_send()
        then_x(d, x).wait_send()
    for d in range(SIZE_X):
        share_y(d, core).wait_send()
        share_x(d, core).wait_send()
    for d in range(1, SIZE_Z):
        there = (z + d) % SIZE_Z

        @pl.when(there < OWNERS)
        def _():
            remote(from_z.at[0], from_z.at[0], send_z.at[d - 1], recv_z.at[d - 1], at_z(d)).wait_send()

    @pl.when(z < OWNERS)
    def _():
        for d in range(1, SIZE_Z // GROUP):
            far(z, d).wait_send()

    for full in (True, False):

        @pl.when((z % GROUP < 2) == full)
        def _():
            for d in range(1, GROUP):
                near(z % GROUP, d, full).wait_send()

    @pl.when((b == 0) & (y == 0))
    def _():
        for d in range(1, SIZE_Y):
            lead(0, d, at_y(d)).wait_send()

    @pl.when(b == 0)
    def _():
        for d in range(1, SIZE_X):
            lead(1, d, at_x(d)).wait_send()

    @pl.when(core == 0)
    def _():
        lead(2, 1, sibling).wait_send()

    for k in range(count):
        for copy in (*first_halo(k), *second_halo(k), to_left(k), to_right(k), on_left(k), on_right(k)):
            copy.wait_send()
        for slot in range(2):
            across(filtered, slot, k).wait_send()


def cholesky(S, work, first, finish):
    row = lax.broadcasted_iota(jnp.int32, (BLOCK, BLOCK), 0)
    column = lax.broadcasted_iota(jnp.int32, (BLOCK, BLOCK), 1)

    def step(k, carry):
        for kk in range(BLOCKS):

            @pl.when(k == kk)
            def _():
                if kk == 0:
                    work[:, 0:BLOCK] = first[...].reshape(BLOCK, BLOCK)
                else:
                    work[:, 0:BLOCK] = S[kk * BLOCK : (kk + 1) * BLOCK, kk * BLOCK : (kk + 1) * BLOCK]

        work[:, BLOCK:] = jnp.where(row == column, 1.0, 0.0)
        factor_diagonal(work)

        @pl.when(k == 0)
        def _():
            finish()

        for kk in range(BLOCKS):

            @pl.when(k == kk)
            def _():
                lo, hi = kk * BLOCK, (kk + 1) * BLOCK
                S[lo:hi, lo:hi] = jnp.where(column >= row, work[:, 0:BLOCK], 0.0)
                if kk < BLOCKS - 1:
                    inverse = jnp.where(column <= row, work[:, BLOCK:], 0.0)
                    S[lo:hi, hi:] = jnp.dot(inverse, S[lo:hi, hi:], precision=HIGHEST, preferred_element_type=jnp.float32)
                    for a in range(kk + 1, BLOCKS):
                        left = S[lo:hi, a * BLOCK : (a + 1) * BLOCK]
                        S[a * BLOCK : (a + 1) * BLOCK, a * BLOCK :] -= lax.dot_general(
                            left, S[lo:hi, a * BLOCK :], (((0,), (0,)), ((), ())),
                            precision=HIGHEST, preferred_element_type=jnp.float32,
                        )

        return carry

    lax.fori_loop(0, BLOCKS, step, 0)
    for a in range(1, BLOCKS):
        S[a * BLOCK : (a + 1) * BLOCK, 0 : a * BLOCK] = jnp.zeros((BLOCK, a * BLOCK), jnp.float32)


def filtered_factor(orbitals, potential, cells):
    dma = pltpu.SemaphoreType.DMA
    field = pltpu.VMEM((2, GY, GX, BLOCK), jnp.float32)
    count = len(CHUNKS)
    return pl.pallas_call(
        functools.partial(factor_kernel, 1.0 / cells),
        out_shape=(
            jax.ShapeDtypeStruct((2, GY, GX, BLOCK), jnp.float32),
            jax.ShapeDtypeStruct((TOTAL, BLOCK), jnp.float32),
        ),
        in_specs=[pl.BlockSpec(memory_space=pltpu.HBM), pl.BlockSpec(memory_space=pltpu.VMEM)],
        out_specs=(pl.BlockSpec(memory_space=pltpu.VMEM), pl.BlockSpec(memory_space=pltpu.VMEM)),
        scratch_shapes=[
            field, field, field, field, field, field, field,
            pltpu.VMEM((KEPT - 1, 2, GY, GX, BLOCK), jnp.float32),
            pltpu.VMEM((GY, GX, BLOCK), jnp.float32),
            pltpu.VMEM((ROWS, BLOCK), jnp.float32),
            pltpu.VMEM((SIZE_Y - 1, PART_Y, BLOCK), jnp.float32),
            pltpu.VMEM((SIZE_Z - 1, PART_Z, BLOCK), jnp.float32),
            pltpu.VMEM((PART_Y, BLOCK), jnp.float32),
            pltpu.VMEM((SIZE_X, 2, SIZE_Y, 3, 2, 2, PART_Z, BLOCK), jnp.float32),
            pltpu.VMEM((TOTAL, TOTAL), jnp.float32),
            pltpu.VMEM((BLOCK, 2 * BLOCK), jnp.float32),
            pltpu.VMEM((2, 2, 2, PART_Z, BLOCK), jnp.float32),
            dma((1,)),
            dma((2, count)), dma((2, count)),
            dma((2, count)), dma((2, count)),
            dma((4, count)), dma((4, count)),
            dma((2, count)), dma((2, count)),
            dma((SIZE_Y - 1,)), dma((SIZE_Y - 1,)),
            dma((SIZE_Z - 1,)), dma((SIZE_Z - 1,)),
            dma((2, GROUP - 1)), dma((2, GROUP - 1)),
            dma((2, SIZE_Y - 1)), dma((2, SIZE_Y - 1)),
            dma((2, SIZE_X - 1)), dma((2, SIZE_X - 1)),
            dma((2, SIZE_X)), dma((2, SIZE_X)),
            dma((3, 3)), dma((3, 3)),
        ],
        compiler_params=pltpu.CompilerParams(
            collective_id=1, has_side_effects=True, vmem_limit_bytes=40 * 1024 * 1024
        ),
        name="filtered_factor",
    )(orbitals, potential)


def local(orbitals, potential):
    cells = orbitals.shape[0] * GY * GX * SIZE_Y * SIZE_Z
    return filtered_factor(orbitals, potential, cells)


def solution(mesh):
    placed = (P("grid", None, None, "orb"), P("grid", None))
    return jax.shard_map(
        local,
        mesh=mesh,
        in_specs=placed,
        out_specs=(P("grid", None, None, "orb"), P(None, "orb")),
        check_vma=False,
    )
```
